256 devices in a mesh: elem: 32 (over y, z), col: 8 (over x, core).
Axes of the slice: x: 4, y: 4, z: 8, core: 2. Of those that a mesh axis runs over, the one named last changes fastest.
Arguments:
- state: float32 [7, 72, 16, 32768], P(None, None, None, ('elem', 'col')), may hold values from -6 to 6
- metric: float32 [2, 16, 32768], P(None, None, ('elem', 'col')), may hold values from 0.5 to 2
- edge_peer: int32 [4, 32768], P(None, ('elem', 'col')), may hold values from 0 to 32767, as said below
- edge_code: int32 [4, 32768], P(None, ('elem', 'col')), may hold values from 0 to 7, as said below
- span_owner: int32 [4096, 1], P(('elem', 'col')), may hold values from 0 to 7; in each aligned block of 16 rows (0 to 15, 16 to 31, ...) at most 3 rows name the same one
- work_class: int32 [16, 32768], P(None, ('elem', 'col')), may hold values from 0 to 3
Outputs:
- new_state: float32 [7, 72, 16, 32768], P(None, None, None, ('elem', 'col'))
- rain_by_owner: float32 [32, 8, 24, 128], P('elem', 'col')
The draws below stay inside these ranges and needn't reach their ends.
Inputs may be any that keep to these rules, and one draw needn't show every extreme that they name: `edge_peer`: elements are numbered device by device along elem+col, 128 to a device. Every edge neighbour lies on the element's own device or on the device directly before or after it along elem+col, which closes into a loop; at most 64 edges of a device's elements meet the next device, and at most as many the previous one. The relation is symmetric: if edge k of element a meets edge k2 of element b, then edge k2 of b meets edge k of a with the same reversal. `edge_code`: the code is 2 k2 + r, where k2 is the neighbour's edge and r is 1 if the two edges number their points in opposite orders. `span_owner`: among the 16 spans of one device no owner is named more than 3 times, and in some device one owner is named exactly 3 times.
All inputs are finite; a program needn't handle non-finite values.
Results may differ from the reference program's by a relative error of at most 0.0003.
Values sent between devices are 32-bit elements; how exact they have to be, the bound alone decides.
No kernel may reach another device: no remote copies, remote signals or barrier semaphores. Data moves between devices by JAX's collectives and lax.ppermute only.
A program may use at most 128 MiB of HBM per device.

```python
import math
import jax
import jax.numpy as jnp
import numpy as np
from jax import lax

ELEM_DEV = 128
LEV = 72
NVAR = 7
SPAN_ELEMS = 8
ELEMS = 32768
SPAN_DEV = 16
CAP = 3
SPANS = 4096
SPAN_COLS = 128
N_ELEM = 32
N_COL = 8


def side_parity(side_list, rotation):
    flip_count = jnp.zeros_like(side_list)
    for section_num in range(3):
        flip_count = flip_count + jnp.where(section_num < rotation, (side_list + section_num) % 2, 0)
    return flip_count % 2


def element_links(key):
    half_rows = ELEM_DEV // 2
    device_count = ELEMS // ELEM_DEV
    row_count = 2 * device_count
    device_keys = jax.random.split(jax.random.fold_in(key, 101), device_count)
    orders = jax.vmap(lambda subkey: jax.random.permutation(subkey, ELEM_DEV))(device_keys).astype(jnp.int32)
    rotation = jax.random.randint(jax.random.fold_in(key, 102), (ELEMS,), 0, 4).astype(jnp.int32)
    grid_index = jnp.arange(ELEMS, dtype=jnp.int32)
    element_id = grid_index // ELEM_DEV * ELEM_DEV + orders.reshape(-1)
    grid_row = grid_index // half_rows
    across = grid_index % half_rows
    side_list = jnp.arange(4, dtype=jnp.int32)[:, None]
    facing = (side_list + rotation[None, :]) % 4
    row_step = jnp.where(facing == 0, -1, jnp.where(facing == 2, 1, 0))
    col_step = jnp.where(facing == 1, 1, jnp.where(facing == 3, -1, 0))
    opposite = (grid_row[None, :] + row_step) % row_count * half_rows + (across[None, :] + col_step) % half_rows
    other_turn = rotation[opposite]
    other_side = (facing + 2 - other_turn) % 4
    reversal = (side_parity(side_list + 0 * opposite, rotation[None, :] + 0 * opposite) + side_parity(other_side, other_turn)) % 2
    codes_out = (2 * other_side + reversal).astype(jnp.int32)
    peers = element_id[opposite].astype(jnp.int32)
    edge_peer = jnp.zeros((4, ELEMS), jnp.int32).at[:, element_id].set(peers)
    edge_code = jnp.zeros((4, ELEMS), jnp.int32).at[:, element_id].set(codes_out)
    return (edge_peer, edge_code)


def draw_edge_peer(key, part):
    links = element_links(key)
    return links[0]


def draw_edge_code(key, part):
    links = element_links(key)
    return links[1]


def draw_work_class(key, part):
    key = jax.random.fold_in(key, 3)
    levels = jax.random.randint(jax.random.fold_in(key, 1), (SPANS,), 0, 4).astype(jnp.int32)
    jitter = jax.random.randint(jax.random.fold_in(key, 2), (16, ELEMS), -1, 2).astype(jnp.int32)
    spread_levels = jnp.repeat(levels, SPAN_ELEMS)[None, :]
    return jnp.clip(spread_levels + jitter, 0, 3).astype(jnp.int32)


def shard_levels(rng, extent, pieces, low, top_value):
    loudness, own = 1.0, jax.random.fold_in(rng, 6)
    for dim, parts in pieces:
        heights = jnp.exp(jax.random.uniform(jax.random.fold_in(own, dim), (parts,), jnp.float32, low / len(pieces), top_value / len(pieces)))
        loudness = loudness * jnp.repeat(heights, extent[dim] // parts).reshape([-1 if axis == dim else 1 for axis in range(len(extent))])
    return loudness


def assign_block(stream_key, own, number, rows, amount, top, reach, skew):
    order = jax.random.permutation(stream_key, amount)
    heavy_load, ordinary = load_shares(amount, rows * top, reach, skew, True), load_shares(amount, rows * top, reach, skew, False)
    places = jnp.arange(amount)

    def named(lengths, offset_by):
        used = int((lengths > 0).sum())
        fixed = max(1, used // 4)
        passed = fixed + (places - fixed + offset_by * (used - fixed)) % max(1, amount - fixed)
        return jnp.zeros((amount,), jnp.int32).at[order[jnp.where(places < fixed, places, passed)]].set(jnp.asarray(lengths, jnp.int32))

    lengths = jnp.where(number % 4 == 0, named(heavy_load, number // 4), named(ordinary, number - number // 4 - 1))
    mixed = jax.random.permutation(jax.random.fold_in(own, 3), amount)
    donor, sink = mixed[0:amount // 2 * 2:2], mixed[1:amount // 2 * 2:2]
    margin = jnp.minimum(lengths[donor] - 1, reach - lengths[sink]) // 2
    margin = jnp.where((donor == order[0]) | (sink == order[0]) | (lengths[sink] == 0), 0, jnp.maximum(margin, 0))
    passed = jax.random.randint(jax.random.fold_in(own, 4), (amount // 2,), 0, 1 << 20) % (margin + 1)
    lengths = lengths.at[donor].add(-passed).at[sink].add(passed)
    labels = jnp.searchsorted(jnp.cumsum(lengths), jnp.arange(rows * top), side="right").astype(jnp.int32)
    grid = labels.reshape(top, rows).T
    grid = grid[jax.random.permutation(jax.random.fold_in(own, 1), rows)]
    offset_by = jax.random.randint(jax.random.fold_in(own, 2), (rows, 1), 0, top)
    return jnp.take_along_axis(grid, (jnp.arange(top)[None, :] + offset_by) % top, axis=1)


def load_shares(amount, total, bound, skew, full):
    weights = [(1 << 20) // math.isqrt(rank ** skew) + 1 for rank in range(1, amount + 1)]
    largest = bound if full else min(bound, max(-(-total // amount), total * weights[0] // sum(weights)))
    least = 1 if total - largest >= amount - 1 else 0
    counts, spare = [largest] + [least] * (amount - 1), total - largest - least * (amount - 1)
    while spare > 0:
        movable = [i for i in range(1, amount) if counts[i] < largest] or [i for i in range(1, amount) if counts[i] < bound]
        pool, remaining = sum([weights[i] for i in movable]), spare
        for i in movable:
            addition = min(bound - counts[i], max(1, remaining * weights[i] // pool), spare)
            counts[i] = counts[i] + addition
            spare = spare - addition
    return np.array(counts)


def centred(own_key, shape, deviation, limit, pieces=(), held_as=jnp.bfloat16):
    drawn = deviation * jax.random.normal(own_key, shape, jnp.float32)
    if pieces:
        drawn = drawn * shard_levels(own_key, shape, pieces, -0.22, 0.18)
    return jnp.clip(drawn, -limit, limit).astype(held_as)


def setup_inputs(seed: int = 0) -> dict:
    keys = jax.random.split(jax.random.key(seed), 7)
    state = centred(keys[0], (NVAR, LEV, 16, ELEMS), 1.0, 6.0, ((3, 256),), jnp.float32)
    metric = jnp.clip(jnp.exp(math.log(2.0) - 1.3862944 * jax.random.uniform(keys[1], (2, 16, ELEMS), jnp.float32) ** shard_levels(keys[1], (2, 16, ELEMS), ((2, 256),), -0.2, 0.2)), 0.5, 2.0)
    edge_peer = draw_edge_peer(jax.random.fold_in(keys[6], 71), 0)
    edge_code = draw_edge_code(jax.random.fold_in(keys[6], 71), 0)
    span_owner_keys = jax.random.split(jax.random.fold_in(keys[4], 1), SPANS // SPAN_DEV)
    span_owner_turns = jax.random.permutation(jax.random.fold_in(keys[4], 3), SPANS // SPAN_DEV)
    span_owner = jax.vmap(lambda own, number: assign_block(jax.random.fold_in(keys[4], 2), own, number, SPAN_DEV, N_COL, 1, CAP, 2))(span_owner_keys, span_owner_turns).reshape((SPANS, 1))
    work_class = draw_work_class(jax.random.fold_in(keys[6], 71), 0)
    return dict(state=state, metric=metric, edge_peer=edge_peer, edge_code=edge_code, span_owner=span_owner, work_class=work_class)


EDGE_POINTS = ((0, 1, 2, 3), (3, 7, 11, 15), (12, 13, 14, 15), (0, 4, 8, 12))
RIM_POINTS = (0, 1, 2, 3, 4, 7, 8, 11, 12, 13, 14, 15)
EDGE_FLAT = (0, 1, 2, 3, 3, 7, 11, 15, 12, 13, 14, 15, 0, 4, 8, 12)
DT_STEP = 0.03

def gll_tables():
    gll_nodes = np.array([-1.0, -1.0 / np.sqrt(5.0), 1.0 / np.sqrt(5.0), 1.0])
    weights = np.array([1.0 / np.prod([gll_nodes[node_a] - gll_nodes[node_b] for node_b in range(4) if node_b != node_a]) for node_a in range(4)])
    derivative = np.zeros((4, 4))
    for node_a in range(4):
        for node_b in range(4):
            if node_a != node_b:
                derivative[node_a, node_b] = weights[node_b] / weights[node_a] / (gll_nodes[node_a] - gll_nodes[node_b])
        derivative[node_a, node_a] = -derivative[node_a].sum()
    along_x = np.kron(np.eye(4), derivative)
    along_y = np.kron(derivative, np.eye(4))
    spread = np.zeros((16, 16))
    for edge_num in range(4):
        for point_num in range(4):
            spread[EDGE_POINTS[edge_num][point_num], 4 * edge_num + point_num] = 1.0
    rim_table = np.array([RIM_POINTS.index(EDGE_POINTS[edge_num][point_num]) for edge_num in range(4) for point_num in range(4)])
    return (jnp.asarray(along_x, jnp.float32), jnp.asarray(along_y, jnp.float32), jnp.asarray(spread, jnp.float32), rim_table)

def local_tendency(fields, metric, along_x, along_y):
    highest = lax.Precision.HIGHEST
    flux_x = metric[0][None, None] * jnp.einsum('pq,vlqe->vlpe', along_x, fields, precision=highest)
    flux_y = metric[1][None, None] * jnp.einsum('pq,vlqe->vlpe', along_y, fields, precision=highest)
    return jnp.einsum('pq,vlqe->vlpe', along_x, flux_x, precision=highest) + jnp.einsum('pq,vlqe->vlpe', along_y, flux_y, precision=highest)

def rim_position(edge_code, rim_table):
    turned = edge_code // 2
    flipped = edge_code % 2
    positions = jnp.arange(4, dtype=jnp.int32)
    along_edge = jnp.where(flipped[:, None, :] == 1, 3 - positions[None, :, None], positions[None, :, None])
    flat_index = (turned[:, None, :] * 4 + along_edge).astype(jnp.int32)
    table = jnp.asarray(rim_table, jnp.int32)
    match = flat_index[..., None] == jnp.arange(16, dtype=jnp.int32)
    return lax.optimization_barrier(jnp.sum(jnp.where(match, table, 0), axis=-1)).astype(jnp.int32)

def smooth_edges(tendency, neighbour, spread):
    own_edge = tendency[:, :, np.asarray(EDGE_FLAT), :]
    return tendency + 0.5 * jnp.einsum('pq,vlqe->vlpe', spread, neighbour - own_edge, precision=lax.Precision.HIGHEST)

def to_spans(values):
    count = values.shape[3] // SPAN_ELEMS
    shaped = values.reshape(values.shape[0], values.shape[1], 16, count, SPAN_ELEMS)
    return shaped.transpose(3, 0, 1, 2, 4).reshape(count, values.shape[0], values.shape[1], SPAN_COLS)

def from_spans(values):
    count = values.shape[0]
    shaped = values.reshape(count, values.shape[1], values.shape[2], 16, SPAN_ELEMS)
    return shaped.transpose(1, 2, 3, 0, 4).reshape(values.shape[1], values.shape[2], 16, count * SPAN_ELEMS)

def span_tags(work_class):
    count = work_class.shape[1] // SPAN_ELEMS
    shaped = work_class.reshape(16, count, SPAN_ELEMS).transpose(1, 0, 2).reshape(count, SPAN_COLS)
    return (shaped + 1).astype(jnp.float32)

def mix_height_layers(profile):
    upper_level = jnp.concatenate([profile[..., :1, :], profile[..., :-1, :]], axis=-2)
    lower_level = jnp.concatenate([profile[..., 1:, :], profile[..., -1:, :]], axis=-2)
    return profile + 0.25 * (upper_level + lower_level - 2.0 * profile)

def column_physics(profile_pile, column_tags):
    atmospheric_heat = profile_pile[..., 0, :, :]
    vapour_ratio = profile_pile[..., 1, :, :]
    droplet_moisture = profile_pile[..., 2, :, :]
    rainfall = jnp.zeros(column_tags.shape, jnp.float32)
    for section_num in (1, 2, 3):
        working_markers = (column_tags > section_num + 0.5).astype(jnp.float32)[..., None, :]
        condensate_mass = working_markers * 0.3 * jax.nn.softplus(vapour_ratio - 0.5 * atmospheric_heat)
        vapour_ratio = vapour_ratio - condensate_mass
        atmospheric_heat = atmospheric_heat + 0.5 * condensate_mass
        droplet_moisture = droplet_moisture + condensate_mass
        rainfall = rainfall + lax.optimization_barrier(jnp.sum(condensate_mass, axis=-2))
    rain = rainfall / LEV * (column_tags > 0.5).astype(jnp.float32)
    mixed_prognostics = jnp.stack([mix_height_layers(atmospheric_heat), mix_height_layers(vapour_ratio), mix_height_layers(droplet_moisture)], axis=-3)
    return (mixed_prognostics - profile_pile, rain)

def reference(state, metric, edge_peer, edge_code, span_owner, work_class):
    along_x, along_y, spread, rim_table = gll_tables()
    tendency = local_tendency(state, metric, along_x, along_y)
    rim_values = tendency[:, :, np.asarray(RIM_POINTS), :]
    variables, levels = (state.shape[0], state.shape[1])
    flat_rim = rim_values.reshape(variables * levels, 12 * ELEMS)
    flat_index = rim_position(edge_code, rim_table) * ELEMS + edge_peer[:, None, :]
    neighbour = jnp.take(flat_rim, flat_index.reshape(-1), axis=1).reshape(variables, levels, 16, ELEMS)
    state_dyn = state + DT_STEP * smooth_edges(tendency, neighbour, spread)
    change, rain = column_physics(to_spans(state_dyn[2:5]), span_tags(work_class))
    new_state = jnp.concatenate([state_dyn[:2], state_dyn[2:5] + from_spans(change), state_dyn[5:]], axis=0)
    device_count = N_ELEM * N_COL
    owners = span_owner[:, 0].reshape(device_count, SPAN_DEV)
    onehot = (owners[:, :, None] == jnp.arange(N_COL, dtype=jnp.int32)).astype(jnp.int32)
    span_rank = lax.optimization_barrier(jnp.sum((jnp.cumsum(onehot, axis=1) - onehot) * onehot, axis=2)).astype(jnp.int32)
    source = jnp.arange(device_count, dtype=jnp.int32)
    target = ((source // N_COL)[:, None] * N_COL + owners).astype(jnp.int32)
    span_slot = ((source % N_COL)[:, None] * CAP + span_rank).astype(jnp.int32)
    slot_table = jnp.zeros((device_count, N_COL * CAP, SPAN_COLS), jnp.float32)
    slot_table = slot_table.at[target.reshape(-1), span_slot.reshape(-1)].set(rain)
    return (new_state, slot_table.reshape(N_ELEM, N_COL, N_COL * CAP, SPAN_COLS))
```

```python
import jax
import jax.numpy as jnp
import numpy as np
from jax import lax
from jax.experimental import pallas as pl
from jax.experimental.pallas import tpu as pltpu
from jax.sharding import PartitionSpec as P

LEV = 72
GROUPS = LEV // 8
ROWS = LEV * 16
LANES = 128
EDGE_POINTS = ((0, 1, 2, 3), (3, 7, 11, 15), (12, 13, 14, 15), (0, 4, 8, 12))
RIM_POINTS = (0, 1, 2, 3, 4, 7, 8, 11, 12, 13, 14, 15)
CORNERS = (0, 3, 12, 15)
SCALE = 0.5 * 0.03
FIRST = (2, 3, 4)
SECOND = (0, 1, 5, 6)
CAP = 3
F32 = jnp.float32
BF16 = jnp.bfloat16
VMEM_LIMIT = 40 * 1024 * 1024


def derivative_matrix():
    nodes = np.array([-1.0, -1.0 / np.sqrt(5.0), 1.0 / np.sqrt(5.0), 1.0])
    weights = np.array(
        [1.0 / np.prod([nodes[a] - nodes[b] for b in range(4) if b != a]) for a in range(4)]
    )
    table = np.zeros((4, 4))
    for a in range(4):
        for b in range(4):
            if a != b:
                table[a, b] = weights[b] / weights[a] / (nodes[a] - nodes[b])
        table[a, a] = -table[a].sum()
    return table


DG = derivative_matrix()
EVEN0 = float((DG[0, 0] + DG[0, 3]) / 2)
EVEN1 = float((DG[1, 0] + DG[1, 3]) / 2)
ODD00 = float((DG[0, 0] - DG[0, 3]) / 2)
ODD01 = float((DG[0, 1] - DG[0, 2]) / 2)
ODD10 = float((DG[1, 0] - DG[1, 3]) / 2)
ODD11 = float((DG[1, 1] - DG[1, 2]) / 2)


def derive(u0, u1, u2, u3):
    even = (u0 + u3) - (u1 + u2)
    o0 = u0 - u3
    o1 = u1 - u2
    a0 = EVEN0 * even
    a1 = EVEN1 * even
    b0 = ODD00 * o0 + ODD01 * o1
    b1 = ODD10 * o0 + ODD11 * o1
    return a0 + b0, a1 + b1, b1 - a1, b0 - a0


def scaled_tendency(u, metric):
    total = [None] * 16
    for b in range(4):
        points = [4 * b + a for a in range(4)]
        flux = derive(*[u[p] for p in points])
        for p, value in zip(points, derive(*[f * metric(0, p) for f, p in zip(flux, points)])):
            total[p] = value
    for a in range(4):
        points = [a + 4 * b for b in range(4)]
        flux = derive(*[u[p] for p in points])
        for p, value in zip(points, derive(*[f * metric(1, p) for f, p in zip(flux, points)])):
            total[p] = total[p] + value
    return total


def edge_rows(peer_ref, code_ref, me, devices):
    rows = []
    for k in range(4):
        peer = peer_ref[k : k + 1, :]
        code = code_ref[k : k + 1, :]
        offset = lax.shift_right_logical(peer, 7) - me
        source = lax.shift_right_logical(code, 1) * LANES + lax.bitwise_and(peer, LANES - 1)
        rows.append(
            dict(
                source=source,
                own=offset == 0,
                after=(offset == 1) | (offset == 1 - devices),
                before=(offset == -1) | (offset == devices - 1),
            )
        )
    return rows


def one_hot(mask):
    return jnp.where(mask, 1.0, 0.0).astype(BF16)


def pack_weights(rows, hit_ref, less_ref, pack_ref):
    number = lax.broadcasted_iota(jnp.int32, (512, LANES), 0)
    for k, row in enumerate(rows):
        hit_ref[:, k * LANES : (k + 1) * LANES] = one_hot((number == row["source"]) & row["before"])
        less_ref[:, k * LANES : (k + 1) * LANES] = one_hot(number < row["source"])
    met = lax.dot_general(
        jnp.ones((16, 512), BF16), hit_ref[...], (((1,), (1,)), ((), ())), preferred_element_type=F32
    )
    before_slot = jnp.dot(met.astype(BF16), less_ref[...], preferred_element_type=F32)
    lane = lax.broadcasted_iota(jnp.int32, (512, LANES), 1)
    for k in range(4):
        less_ref[:, k * LANES : (k + 1) * LANES] = one_hot(number < lane + k * LANES)
    meets = jnp.concatenate([jnp.where(row["after"], 1.0, 0.0) for row in rows], axis=1)
    after_slot = jnp.dot(
        jnp.broadcast_to(meets, (16, 512)).astype(BF16), less_ref[...], preferred_element_type=F32
    )
    slot = lax.broadcasted_iota(jnp.int32, (64, LANES), 0)
    zero = jnp.zeros((64, LANES), BF16)
    for k, row in enumerate(rows):
        low = slice(k * LANES, (k + 1) * LANES)
        high = slice(512 + k * LANES, 512 + (k + 1) * LANES)
        after = one_hot((slot == after_slot[0:1, low].astype(jnp.int32)) & row["after"])
        before = one_hot((slot == before_slot[0:1, low].astype(jnp.int32)) & row["before"])
        pack_ref[0:64, low] = after
        pack_ref[0:64, high] = zero
        pack_ref[64:128, low] = zero
        pack_ref[64:128, high] = after
        pack_ref[128:192, low] = before
        pack_ref[128:192, high] = zero
        pack_ref[192:256, low] = zero
        pack_ref[192:256, high] = before


def edges_out(count, state_ref, metric_ref, pack_ref, acc_ref, high_ref, low_ref, after_ref, before_ref):
    def metric(direction, point):
        return jnp.broadcast_to(
            SCALE * metric_ref[16 * direction + point : 16 * direction + point + 1, :], (8, LANES)
        )

    def group(index, carry):
        base = index * 128
        u = [state_ref[pl.ds(base + p, 8, stride=16), :] for p in range(16)]
        tendency = scaled_tendency(u, metric)
        for p in range(16):
            if p in CORNERS:
                value = u[p]
            elif p in RIM_POINTS:
                value = u[p] + tendency[p]
            else:
                value = u[p] + 2.0 * tendency[p]
            acc_ref[pl.ds(pl.multiple_of(base + 8 * p, 8), 8), :] = value
        top = {p: tendency[p].astype(BF16).astype(F32) for p in RIM_POINTS}
        rest = {p: tendency[p] - top[p] for p in RIM_POINTS}
        rows = pl.ds(pl.multiple_of(index * 16, 16), 16)
        for k in range(4):
            for half in range(2):
                first, second = EDGE_POINTS[k][2 * half : 2 * half + 2]
                place = slice(half * 512 + k * LANES, half * 512 + (k + 1) * LANES)
                high_ref[rows, place] = jnp.concatenate([top[first], top[second]], 0).astype(BF16)
                low_ref[rows, place] = jnp.concatenate([rest[first], rest[second]], 0).astype(BF16)
        return carry

    lax.fori_loop(0, count * GROUPS, group, 0)
    across = (((1,), (1,)), ((), ()))
    packed = lax.dot_general(
        high_ref[...], pack_ref[...], across, preferred_element_type=F32
    ) + lax.dot_general(low_ref[...], pack_ref[...], across, preferred_element_type=F32)
    after_ref[...] = packed[:, :LANES]
    before_ref[...] = packed[:, LANES:]


def first_kernel(devices, state_ref, metric_ref, peer_ref, code_ref,
                 acc_ref, high_ref, low_ref, pack_ref, after_ref, before_ref,
                 held_ref, hit_ref, less_ref, sem):
    me = lax.axis_index(("elem", "col"))
    copy = pltpu.make_async_copy(
        state_ref.at[pl.ds(FIRST[0] * ROWS, len(FIRST) * ROWS)], held_ref, sem
    )
    copy.start()
    pack_weights(edge_rows(peer_ref, code_ref, me, devices), hit_ref, less_ref, pack_ref)
    copy.wait()
    edges_out(len(FIRST), held_ref, metric_ref, pack_ref, acc_ref, high_ref, low_ref, after_ref, before_ref)


def second_kernel(devices, state_ref, metric_ref, peer_ref, code_ref, pack_ref,
                  acc_ref, high_ref, low_ref, own_ref, after_ref, before_ref,
                  held_ref, sems):
    me = lax.axis_index(("elem", "col"))
    copies = [
        pltpu.make_async_copy(
            state_ref.at[pl.ds(0, 2 * ROWS)], held_ref.at[pl.ds(0, 2 * ROWS)], sems.at[0]
        ),
        pltpu.make_async_copy(
            state_ref.at[pl.ds(5 * ROWS, 2 * ROWS)], held_ref.at[pl.ds(2 * ROWS, 2 * ROWS)], sems.at[1]
        ),
    ]
    for copy in copies:
        copy.start()
    number = lax.broadcasted_iota(jnp.int32, (512, LANES), 0)
    for k, row in enumerate(edge_rows(peer_ref, code_ref, me, devices)):
        own_ref[:, k * LANES : (k + 1) * LANES] = one_hot((number == row["source"]) & row["own"])
    for copy in copies:
        copy.wait()
    edges_out(len(SECOND), held_ref, metric_ref, pack_ref, acc_ref, high_ref, low_ref, after_ref, before_ref)


def split(value):
    top = value.astype(BF16)
    return top, (value - top.astype(F32)).astype(BF16)


def averaged(count, code_ref, acc_ref, high_ref, low_ref, own_ref, pack_ref, from_before_ref,
             from_after_ref, lines_ref, dyn_ref):
    top_next, rest_next = split(from_after_ref[...])
    top_last, rest_last = split(from_before_ref[...])
    top = jnp.concatenate([top_next, top_last], axis=1)
    rest = jnp.concatenate([rest_next, rest_last], axis=1)
    for half in range(2):
        place = slice(half * 512, (half + 1) * 512)
        lines_ref[:, place] = (
            jnp.dot(high_ref[:, place], own_ref[...], preferred_element_type=F32)
            + jnp.dot(low_ref[:, place], own_ref[...], preferred_element_type=F32)
            + jnp.dot(top, pack_ref[:, place], preferred_element_type=F32)
            + jnp.dot(rest, pack_ref[:, place], preferred_element_type=F32)
        )
    turned = [
        jnp.broadcast_to(lax.bitwise_and(code_ref[k : k + 1, :], 1), (8, LANES)) == 1 for k in range(4)
    ]

    def group(index, carry):
        base = index * 128
        value = [acc_ref[pl.ds(pl.multiple_of(base + 8 * p, 8), 8), :] for p in range(16)]
        for k in range(4):
            line = []
            for half in range(2):
                place = slice(half * 512 + k * LANES, half * 512 + (k + 1) * LANES)
                for second in range(2):
                    rows = pl.ds(pl.multiple_of(index * 16 + 8 * second, 8), 8)
                    line.append(lines_ref[rows, place])
            for t in range(4):
                p = EDGE_POINTS[k][t]
                value[p] = value[p] + jnp.where(turned[k], line[3 - t], line[t])
        for p in range(16):
            dyn_ref[pl.ds(base + p, 8, stride=16), :] = value[p]
        return carry

    lax.fori_loop(0, count * GROUPS, group, 0)


def softplus(x):
    tail = jnp.exp(-jnp.abs(x))
    small = tail - 0.5 * tail * tail
    return jnp.maximum(x, 0.0) + jnp.where(tail < 1e-3, small, jnp.log(1.0 + tail))


UNROLL = 8


def physics(dyn_ref, mark_ref):
    work = mark_ref[...]
    marks = [jnp.where(work >= section, 0.3, 0.0) for section in (1, 2, 3)]

    def condense(block, rain):
        base = pl.multiple_of(block * (16 * UNROLL), 16)
        for step in range(UNROLL):
            heat_at = pl.ds(base + 16 * step, 16)
            vapour_at = pl.ds(ROWS + base + 16 * step, 16)
            water_at = pl.ds(2 * ROWS + base + 16 * step, 16)
            heat = dyn_ref[heat_at, :]
            vapour = dyn_ref[vapour_at, :]
            excess = vapour - 0.5 * heat
            total = None
            for mark in marks:
                amount = mark * softplus(excess)
                excess = excess - 1.25 * amount
                total = amount if total is None else total + amount
            dyn_ref[heat_at, :] = heat + 0.5 * total
            dyn_ref[vapour_at, :] = vapour - total
            dyn_ref[water_at, :] = dyn_ref[water_at, :] + total
            rain = rain + total
        return rain

    return lax.fori_loop(0, LEV // UNROLL, condense, jnp.zeros((16, LANES), F32))


def mixed(dyn_ref, out_ref):
    for var in range(3):
        start = var * ROWS

        def at(level, start=start):
            return dyn_ref[pl.ds(start + 16 * level, 16), :]

        upper = here = at(0)
        for level in range(LEV):
            lower = at(min(level + 1, LEV - 1))
            out_ref[pl.ds(start + 16 * level, 16), :] = 0.5 * here + 0.25 * (upper + lower)
            upper, here = here, lower


def by_span(rain):
    point = lax.broadcasted_iota(jnp.int32, (16, LANES), 0)
    eighth = lax.shift_right_logical(lax.broadcasted_iota(jnp.int32, (16, LANES), 1), 3)
    total = None
    for shift in range(16):
        moved = pltpu.roll(rain, 8 * shift, 1) if shift else rain
        kept = jnp.where(point == eighth, moved, 0.0)
        kept = pltpu.roll(kept, 16 - shift, 0) if shift else kept
        total = kept if total is None else total + kept
    return total


def third_kernel(owner_ref, code_ref, mark_ref, acc_ref, high_ref, low_ref, own_ref, pack_ref,
                 from_before_ref, from_after_ref, state_out, rain_ref,
                 lines_ref, dyn_ref, mixed_ref, rain_rows, counts, sem):
    averaged(len(FIRST), code_ref, acc_ref, high_ref, low_ref, own_ref, pack_ref, from_before_ref,
             from_after_ref, lines_ref, dyn_ref)
    rain = physics(dyn_ref, mark_ref)
    mixed(dyn_ref, mixed_ref)
    copy = pltpu.make_async_copy(
        mixed_ref, state_out.at[pl.ds(FIRST[0] * ROWS, len(FIRST) * ROWS)], sem
    )
    copy.start()
    rain_rows[...] = by_span(rain) * (1.0 / LEV)
    rain_ref[...] = jnp.zeros_like(rain_ref)
    for owner in range(8):
        counts[owner] = 0
    for span in range(16):
        owner = owner_ref[span]
        rank = counts[owner]
        counts[owner] = rank + 1
        rain_ref[pl.ds(owner * CAP + rank, 1), :] = rain_rows[span : span + 1, :]
    copy.wait()


def fourth_kernel(code_ref, acc_ref, high_ref, low_ref, own_ref, pack_ref, from_before_ref,
                  from_after_ref, state_in, state_out, lines_ref, dyn_ref, sems):
    del state_in
    averaged(len(SECOND), code_ref, acc_ref, high_ref, low_ref, own_ref, pack_ref, from_before_ref,
             from_after_ref, lines_ref, dyn_ref)
    copies = [
        pltpu.make_async_copy(
            dyn_ref.at[pl.ds(0, 2 * ROWS)], state_out.at[pl.ds(0, 2 * ROWS)], sems.at[0]
        ),
        pltpu.make_async_copy(
            dyn_ref.at[pl.ds(2 * ROWS, 2 * ROWS)], state_out.at[pl.ds(5 * ROWS, 2 * ROWS)], sems.at[1]
        ),
    ]
    for copy in copies:
        copy.start()
    for copy in copies:
        copy.wait()


def passed_along(value, axis, steps):
    count = lax.axis_size(axis)
    pairs = [(source, (source + steps) % count) for source in range(count)]
    return lax.ppermute(value, axis, pairs)


VM = pl.BlockSpec(memory_space=pltpu.VMEM)
SM = pl.BlockSpec(memory_space=pltpu.SMEM)
ANY = pl.BlockSpec(memory_space=pl.ANY)


def shape(*sizes, dtype=F32):
    return jax.ShapeDtypeStruct(sizes, dtype)


def call(kernel, out, ins, outs, scratch, cost, **more):
    return pl.pallas_call(
        kernel,
        out_shape=out,
        in_specs=ins,
        out_specs=outs,
        scratch_shapes=scratch,
        cost_estimate=pl.CostEstimate(flops=cost, bytes_accessed=4 << 20, transcendentals=0),
        compiler_params=pltpu.CompilerParams(vmem_limit_bytes=VMEM_LIMIT),
        **more,
    )


def body(state, metric, edge_peer, edge_code, span_owner, work_class):
    axes = ("elem", "col")
    devices = lax.axis_size(axes)
    state = state.reshape(7 * ROWS, LANES)
    metric = metric.reshape(32, LANES)
    owner = span_owner.reshape(16)
    n1, n2 = len(FIRST), len(SECOND)

    def sizes(count):
        return [
            shape(count * ROWS, LANES),
            shape(count * 144, 1024, dtype=BF16),
            shape(count * 144, 1024, dtype=BF16),
        ]

    acc1, high1, low1, pack, after1, before1 = call(
        lambda *refs: first_kernel(devices, *refs),
        sizes(n1) + [shape(256, 1024, dtype=BF16), shape(n1 * 144, LANES), shape(n1 * 144, LANES)],
        [ANY, VM, VM, VM],
        [VM] * 6,
        [
            pltpu.VMEM((n1 * ROWS, LANES), F32),
            pltpu.VMEM((512, 512), BF16),
            pltpu.VMEM((512, 512), BF16),
            pltpu.SemaphoreType.DMA,
        ],
        500_000_000,
    )(state, metric, edge_peer, edge_code)
    from_before1 = passed_along(after1, axes, 1)
    from_after1 = passed_along(before1, axes, -1)
    acc2, high2, low2, own, after2, before2 = call(
        lambda *refs: second_kernel(devices, *refs),
        sizes(n2) + [shape(512, 512, dtype=BF16), shape(n2 * 144, LANES), shape(n2 * 144, LANES)],
        [ANY, VM, VM, VM, VM],
        [VM] * 6,
        [pltpu.VMEM((n2 * ROWS, LANES), F32), pltpu.SemaphoreType.DMA((2,))],
        500_000_000,
    )(state, metric, edge_peer, edge_code, pack)
    from_before2 = passed_along(after2, axes, 1)
    from_after2 = passed_along(before2, axes, -1)
    new_state, rain = call(
        third_kernel,
        [shape(7 * ROWS, LANES), shape(8 * CAP, LANES)],
        [SM] + [VM] * 9,
        [ANY, VM],
        [
            pltpu.VMEM((n1 * 144, 1024), F32),
            pltpu.VMEM((n1 * ROWS, LANES), F32),
            pltpu.VMEM((n1 * ROWS, LANES), F32),
            pltpu.VMEM((16, LANES), F32),
            pltpu.SMEM((8,), jnp.int32),
            pltpu.SemaphoreType.DMA,
        ],
        2_000_000_000,
    )(
        owner, edge_code, work_class, acc1, high1, low1, own, pack, from_before1, from_after1
    )
    rain = lax.all_to_all(rain.reshape(8, CAP, LANES), "col", split_axis=0, concat_axis=0, tiled=True)
    new_state = call(
        fourth_kernel,
        shape(7 * ROWS, LANES),
        [VM] * 8 + [ANY],
        ANY,
        [
            pltpu.VMEM((n2 * 144, 1024), F32),
            pltpu.VMEM((n2 * ROWS, LANES), F32),
            pltpu.SemaphoreType.DMA((2,)),
        ],
        2_000_000_000,
        input_output_aliases={8: 0},
    )(edge_code, acc2, high2, low2, own, pack, from_before2, from_after2, new_state)
    return new_state.reshape(7, LEV, 16, LANES), rain.reshape(1, 1, 8 * CAP, LANES)


def solution(mesh):
    placed = (
        P(None, None, None, ("elem", "col")),
        P(None, None, ("elem", "col")),
        P(None, ("elem", "col")),
        P(None, ("elem", "col")),
        P(("elem", "col"), None),
        P(None, ("elem", "col")),
    )
    return jax.shard_map(
        body,
        mesh=mesh,
        in_specs=placed,
        out_specs=(P(None, None, None, ("elem", "col")), P("elem", "col", None, None)),
        check_vma=False,
    )
```

```python
import jax
import jax.numpy as jnp
import numpy as np
from jax import lax
from jax.experimental import pallas as pl
from jax.experimental.pallas import tpu as pltpu
from jax.sharding import PartitionSpec as P

LEV = 72
GROUPS = LEV // 8
ROWS = LEV * 16
LANES = 128
EDGE_POINTS = ((0, 1, 2, 3), (3, 7, 11, 15), (12, 13, 14, 15), (0, 4, 8, 12))
RIM_POINTS = (0, 1, 2, 3, 4, 7, 8, 11, 12, 13, 14, 15)
CORNERS = (0, 3, 12, 15)
SCALE = 0.5 * 0.03
ORDER = (2, 3, 4, 0, 1, 5, 6)
NVAR = 7
LINES = NVAR * GROUPS * 16
CAP = 3
F32 = jnp.float32
BF16 = jnp.bfloat16
VMEM_LIMIT = 20 * 1024 * 1024


def derivative_matrix():
    nodes = np.array([-1.0, -1.0 / np.sqrt(5.0), 1.0 / np.sqrt(5.0), 1.0])
    weights = np.array(
        [1.0 / np.prod([nodes[a] - nodes[b] for b in range(4) if b != a]) for a in range(4)]
    )
    table = np.zeros((4, 4))
    for a in range(4):
        for b in range(4):
            if a != b:
                table[a, b] = weights[b] / weights[a] / (nodes[a] - nodes[b])
        table[a, a] = -table[a].sum()
    return table


DG = derivative_matrix()
EVEN0 = float((DG[0, 0] + DG[0, 3]) / 2)
EVEN1 = float((DG[1, 0] + DG[1, 3]) / 2)
ODD00 = float((DG[0, 0] - DG[0, 3]) / 2)
ODD01 = float((DG[0, 1] - DG[0, 2]) / 2)
ODD10 = float((DG[1, 0] - DG[1, 3]) / 2)
ODD11 = float((DG[1, 1] - DG[1, 2]) / 2)


def derive_fluxes(u0, u1, u2, u3):
    even = (u0 + u3) - (u1 + u2)
    o0 = u0 - u3
    o1 = u1 - u2
    b0 = (ODD00 / EVEN0) * o0 + (ODD01 / EVEN0) * o1
    b1 = (ODD10 / EVEN1) * o0 + (ODD11 / EVEN1) * o1
    return even + b0, even + b1, b1 - even, b0 - even


def derive_again(u0, u1, u2, u3):
    even = (u0 + u3) - (u1 + u2)
    o0 = u0 - u3
    o1 = u1 - u2
    a1 = (EVEN1 / EVEN0) * even
    b0 = (ODD00 / EVEN0) * o0 + (ODD01 / EVEN0) * o1
    b1 = (ODD10 / EVEN0) * o0 + (ODD11 / EVEN0) * o1
    return even + b0, a1 + b1, b1 - a1, b0 - even


def metric_scale(direction, point):
    row = (point // 4, point % 4)[1 - direction]
    return SCALE * EVEN0 * (EVEN0, EVEN1, EVEN1, EVEN0)[row]


def scaled_tendency(u, metric):
    total = [None] * 16
    for b in range(4):
        points = [4 * b + a for a in range(4)]
        flux = derive_fluxes(*[u[p] for p in points])
        for p, value in zip(points, derive_again(*[f * metric(0, p) for f, p in zip(flux, points)])):
            total[p] = value
    for a in range(4):
        points = [a + 4 * b for b in range(4)]
        flux = derive_fluxes(*[u[p] for p in points])
        for p, value in zip(points, derive_again(*[f * metric(1, p) for f, p in zip(flux, points)])):
            total[p] = total[p] + value
    return total


def edge_rows(peer_ref, code_ref, me, devices):
    rows = []
    for k in range(4):
        peer = peer_ref[k : k + 1, :]
        code = code_ref[k : k + 1, :]
        offset = lax.shift_right_logical(peer, 7) - me
        source = lax.shift_right_logical(code, 1) * LANES + lax.bitwise_and(peer, LANES - 1)
        rows.append(
            dict(
                source=source,
                own=offset == 0,
                after=(offset == 1) | (offset == 1 - devices),
                before=(offset == -1) | (offset == devices - 1),
            )
        )
    return rows


def one_hot(mask):
    return jnp.where(mask, 1.0, 0.0).astype(BF16)


def pack_weights(rows, even, hit_ref, less_ref, pack_ref, halo_ref):
    number = lax.broadcasted_iota(jnp.int32, (512, LANES), 0)
    for k, row in enumerate(rows):
        hit_ref[:, k * LANES : (k + 1) * LANES] = one_hot((number == row["source"]) & row["before"])
        less_ref[:, k * LANES : (k + 1) * LANES] = one_hot(number < row["source"])
    met = lax.dot_general(
        jnp.ones((16, 512), BF16), hit_ref[...], (((1,), (1,)), ((), ())), preferred_element_type=F32
    )
    before_slot = jnp.dot(met.astype(BF16), less_ref[...], preferred_element_type=F32)
    lane = lax.broadcasted_iota(jnp.int32, (512, LANES), 1)
    for k in range(4):
        less_ref[:, k * LANES : (k + 1) * LANES] = one_hot(number < lane + k * LANES)
    meets = jnp.concatenate([jnp.where(row["after"], 1.0, 0.0) for row in rows], axis=1)
    after_slot = jnp.dot(
        jnp.broadcast_to(meets, (16, 512)).astype(BF16), less_ref[...], preferred_element_type=F32
    )
    slot = lax.broadcasted_iota(jnp.int32, (64, LANES), 0)
    zero = jnp.zeros((64, LANES), BF16)
    for k, row in enumerate(rows):
        low = slice(k * LANES, (k + 1) * LANES)
        high = slice(512 + k * LANES, 512 + (k + 1) * LANES)
        after = jnp.where(row["after"], after_slot[0:1, low], -1.0).astype(jnp.int32)
        before = jnp.where(row["before"], before_slot[0:1, low], -1.0).astype(jnp.int32)
        near = one_hot(slot == jnp.where(even, after, before))
        far = one_hot(slot == jnp.where(even, before, after))
        pack_ref[0:64, low] = near
        pack_ref[0:64, high] = zero
        pack_ref[64:128, low] = zero
        pack_ref[64:128, high] = near
        pack_ref[128:192, low] = zero
        pack_ref[128:192, high] = far
        pack_ref[192:256, low] = far
        pack_ref[192:256, high] = zero
        for again in (0, 128):
            halo_ref[again : again + 64, low] = near
            halo_ref[again + 64 : again + 128, low] = far
            halo_ref[again : again + 64, high] = far
            halo_ref[again + 64 : again + 128, high] = near


def edges_out(state_ref, metric_ref, pack_ref, acc_ref, high_ref, low_ref, near_ref, far_ref, ready):
    def metric(direction, point):
        row = 8 * (16 * direction + point)
        return metric_ref[row : row + 8, :]

    def group(index, carry):
        base = index * 128
        u = [state_ref[pl.ds(base + p, 8, stride=16), :] for p in range(16)]
        tendency = scaled_tendency(u, metric)
        for p in range(16):
            if p in CORNERS:
                value = u[p]
            elif p in RIM_POINTS:
                value = u[p] + tendency[p]
            else:
                value = u[p] + 2.0 * tendency[p]
            acc_ref[pl.ds(pl.multiple_of(base + 8 * p, 8), 8), :] = value
        top = {p: tendency[p].astype(BF16).astype(F32) for p in RIM_POINTS}
        rest = {p: tendency[p] - top[p] for p in RIM_POINTS}
        rows = pl.ds(pl.multiple_of(index * 16, 16), 16)
        for k in range(4):
            for half in range(2):
                first, second = EDGE_POINTS[k][2 * half : 2 * half + 2]
                place = slice(half * 512 + k * LANES, half * 512 + (k + 1) * LANES)
                high_ref[rows, place] = jnp.concatenate([top[first], top[second]], 0).astype(BF16)
                low_ref[rows, place] = jnp.concatenate([rest[first], rest[second]], 0).astype(BF16)
        return carry

    for var in range(NVAR):
        ready(var)
        lax.fori_loop(var * GROUPS, (var + 1) * GROUPS, group, 0)
    across = (((1,), (1,)), ((), ()))
    packed = lax.dot_general(
        high_ref[...], pack_ref[...], across, preferred_element_type=F32
    ) + lax.dot_general(low_ref[...], pack_ref[...], across, preferred_element_type=F32)
    near_ref[...] = packed[:, :LANES]
    far_ref[...] = packed[:, LANES:]


def first_kernel(devices, state_hbm, metric_hbm, peer_hbm, code_hbm, work_hbm,
                 code_ref, work_ref, own_ref, halo_ref, acc_ref, high_ref, low_ref, near_ref, far_ref,
                 state_ref, metric_ref, scaled_ref, peer_ref, hit_ref, less_ref, pack_ref, sems):
    me = lax.axis_index(("elem", "col"))
    small = [
        pltpu.make_async_copy(source, target, sems.at[NVAR + i])
        for i, (source, target) in enumerate(
            [(peer_hbm, peer_ref), (code_hbm, code_ref), (metric_hbm, metric_ref), (work_hbm, work_ref)]
        )
    ]
    large = [
        pltpu.make_async_copy(
            state_hbm.at[pl.ds(var * ROWS, ROWS)], state_ref.at[pl.ds(i * ROWS, ROWS)], sems.at[i]
        )
        for i, var in enumerate(ORDER)
    ]
    for copy in small + large:
        copy.start()
    small[0].wait()
    small[1].wait()
    rows = edge_rows(peer_ref, code_ref, me, devices)
    pack_weights(rows, lax.rem(me, 2) == 0, hit_ref, less_ref, pack_ref, halo_ref)
    number = lax.broadcasted_iota(jnp.int32, (512, LANES), 0)
    for k, row in enumerate(rows):
        own_ref[:, k * LANES : (k + 1) * LANES] = one_hot((number == row["source"]) & row["own"])
    small[2].wait()
    small[3].wait()
    for i in range(32):
        scaled_ref[8 * i : 8 * i + 8, :] = jnp.broadcast_to(
            metric_scale(i // 16, i % 16) * metric_ref[i : i + 1, :], (8, LANES)
        )
    edges_out(state_ref, scaled_ref, pack_ref, acc_ref, high_ref, low_ref, near_ref, far_ref,
              lambda i: large[i].wait())


def split(value):
    top = value.astype(BF16)
    return top, (value - top.astype(F32)).astype(BF16)


def turned_edges(code_ref):
    return [
        jnp.broadcast_to(lax.bitwise_and(code_ref[k : k + 1, :], 1), (8, LANES)) == 1 for k in range(4)
    ]


def averaged(index, turned, acc_ref, lines_ref):
    base = index * 128
    value = [acc_ref[pl.ds(pl.multiple_of(base + 8 * p, 8), 8), :] for p in range(16)]
    for k in range(4):
        line = []
        for half in range(2):
            place = slice(half * 512 + k * LANES, half * 512 + (k + 1) * LANES)
            for second in range(2):
                rows = pl.ds(pl.multiple_of(index * 16 + 8 * second, 8), 8)
                line.append(lines_ref[rows, place])
        for t in range(4):
            p = EDGE_POINTS[k][t]
            value[p] = value[p] + jnp.where(turned[k], line[3 - t], line[t])
    return value


def second_kernel(code_ref, acc_ref, high_ref, low_ref, own_ref, out_ref, lines_ref):
    for half in range(2):
        place = slice(half * 512, (half + 1) * 512)
        lines_ref[:, place] = jnp.dot(
            high_ref[:, place], own_ref[...], preferred_element_type=F32
        ) + jnp.dot(low_ref[:, place], own_ref[...], preferred_element_type=F32)
    turned = turned_edges(code_ref)

    def group(index, carry):
        for p, value in enumerate(averaged(index, turned, acc_ref, lines_ref)):
            out_ref[pl.ds(pl.multiple_of(index * 128 + 8 * p, 8), 8), :] = value
        return carry

    lax.fori_loop(0, NVAR * GROUPS, group, 0)


def softplus(x):
    tail = jnp.exp(-jnp.abs(x))
    small = tail - 0.5 * tail * tail
    return jnp.maximum(x, 0.0) + jnp.where(tail < 1e-3, small, jnp.log(1.0 + tail))


UNROLL = 8


def physics(dyn_ref, mark_ref):
    work = mark_ref[...]
    marks = [jnp.where(work >= section, 0.3, 0.0) for section in (1, 2, 3)]

    def condense(block, rain):
        base = pl.multiple_of(block * (16 * UNROLL), 16)
        for step in range(UNROLL):
            heat_at = pl.ds(base + 16 * step, 16)
            vapour_at = pl.ds(ROWS + base + 16 * step, 16)
            water_at = pl.ds(2 * ROWS + base + 16 * step, 16)
            heat = dyn_ref[heat_at, :]
            vapour = dyn_ref[vapour_at, :]
            excess = vapour - 0.5 * heat
            total = None
            for mark in marks:
                amount = mark * softplus(excess)
                excess = excess - 1.25 * amount
                total = amount if total is None else total + amount
            dyn_ref[heat_at, :] = heat + 0.5 * total
            dyn_ref[vapour_at, :] = vapour - total
            dyn_ref[water_at, :] = dyn_ref[water_at, :] + total
            rain = rain + total
        return rain

    return lax.fori_loop(0, LEV // UNROLL, condense, jnp.zeros((16, LANES), F32))


def mixed(dyn_ref, out_ref):
    for var in range(3):
        start = var * ROWS

        def at(level, start=start):
            return dyn_ref[pl.ds(start + 16 * level, 16), :]

        upper = here = at(0)
        for level in range(LEV):
            lower = at(min(level + 1, LEV - 1))
            out_ref[pl.ds(start + 16 * level, 16), :] = 0.5 * here + 0.25 * (upper + lower)
            upper, here = here, lower


def by_span(rain):
    point = lax.broadcasted_iota(jnp.int32, (16, LANES), 0)
    eighth = lax.shift_right_logical(lax.broadcasted_iota(jnp.int32, (16, LANES), 1), 3)
    total = None
    for shift in range(16):
        moved = pltpu.roll(rain, 8 * shift, 1) if shift else rain
        kept = jnp.where(point == eighth, moved, 0.0)
        kept = pltpu.roll(kept, 16 - shift, 0) if shift else kept
        total = kept if total is None else total + kept
    return total


def halo_lines(first, count, near_ref, far_ref, halo_ref, lines_ref):
    rows = slice(first * 144, (first + count) * 144)
    lane = lax.broadcasted_iota(jnp.int32, (count * 144, LANES), 1)
    for half in range(2):
        low, high = near_ref[rows, :], far_ref[rows, :]
        if half:
            low, high = high, low
        halo = jnp.concatenate(split(jnp.where(lane < 64, low, high)), axis=1)
        place = slice(half * 512, (half + 1) * 512)
        lines_ref[rows, place] = jnp.dot(halo, halo_ref[:, place], preferred_element_type=F32)


def third_kernel(owner_ref, code_ref, mark_ref, acc_ref, halo_ref, near_ref, far_ref,
                 mixed_ref, rain_ref,
                 lines_ref, dyn_ref, rain_rows, counts):
    halo_lines(0, 3, near_ref, far_ref, halo_ref, lines_ref)
    turned = turned_edges(code_ref)

    def group(index, carry):
        for p, value in enumerate(averaged(index, turned, acc_ref, lines_ref)):
            dyn_ref[pl.ds(index * 128 + p, 8, stride=16), :] = value
        return carry

    lax.fori_loop(0, 3 * GROUPS, group, 0)
    rain = physics(dyn_ref, mark_ref)
    mixed(dyn_ref, mixed_ref)
    rain_rows[...] = by_span(rain) * (1.0 / LEV)
    rain_ref[...] = jnp.zeros_like(rain_ref)
    for owner in range(8):
        counts[owner] = 0
    for span in range(16):
        owner = owner_ref[span]
        rank = counts[owner]
        counts[owner] = rank + 1
        rain_ref[pl.ds(owner * CAP + rank, 1), :] = rain_rows[span : span + 1, :]


def fourth_kernel(code_ref, acc_ref, halo_ref, near_ref, far_ref, mixed_ref, state_out,
                  lines_ref, dyn_ref, sems):
    def leave(i, source, start):
        return pltpu.make_async_copy(
            source.at[pl.ds(start, ROWS)], state_out.at[pl.ds(ORDER[i] * ROWS, ROWS)], sems.at[i]
        )

    copies = [leave(i, mixed_ref, i * ROWS) for i in range(3)]
    for copy in copies:
        copy.start()
    halo_lines(3, NVAR - 3, near_ref, far_ref, halo_ref, lines_ref)
    turned = turned_edges(code_ref)

    def group(index, carry):
        for p, value in enumerate(averaged(index, turned, acc_ref, lines_ref)):
            dyn_ref[pl.ds(index * 128 + p, 8, stride=16), :] = value
        return carry

    for i in range(3, NVAR):
        lax.fori_loop(i * GROUPS, (i + 1) * GROUPS, group, 0)
        copies.append(leave(i, dyn_ref, i * ROWS))
        copies[-1].start()
    for copy in copies:
        copy.wait()


def fifth_kernel(all_ref, rain_ref):
    me = lax.axis_index("col")
    for source in range(8):
        rain_ref[CAP * source : CAP * (source + 1), :] = all_ref[pl.ds(8 * CAP * source + CAP * me, CAP), :]


def swapped(value, axes, partner):
    count = lax.axis_size(axes)
    return lax.ppermute(value, axes, [(source, partner(source, count)) for source in range(count)])


def near_partner(source, count):
    return source + 1 if source % 2 == 0 else source - 1


def far_partner(source, count):
    return (source - 1) % count if source % 2 == 0 else (source + 1) % count


VM = pl.BlockSpec(memory_space=pltpu.VMEM)
SM = pl.BlockSpec(memory_space=pltpu.SMEM)
HB = pl.BlockSpec(memory_space=pltpu.HBM)


def shape(*sizes, dtype=F32):
    return jax.ShapeDtypeStruct(sizes, dtype)


def call(kernel, out, ins, outs, scratch, cost, **more):
    return pl.pallas_call(
        kernel,
        out_shape=out,
        in_specs=ins,
        out_specs=outs,
        scratch_shapes=scratch,
        cost_estimate=pl.CostEstimate(flops=cost, bytes_accessed=4 << 20, transcendentals=0),
        compiler_params=pltpu.CompilerParams(vmem_limit_bytes=VMEM_LIMIT),
        **more,
    )


def in_hbm(value):
    return pltpu.with_memory_space_constraint(value, pltpu.HBM)


def body(state, metric, edge_peer, edge_code, span_owner, work_class):
    axes = ("elem", "col")
    devices = lax.axis_size(axes)
    state = state.reshape(NVAR * ROWS, LANES)
    metric = metric.reshape(32, LANES)
    owner = span_owner.reshape(16)
    code, work, own, halo, acc, high, low, near, far = call(
        lambda *refs: first_kernel(devices, *refs),
        [
            shape(4, LANES, dtype=jnp.int32),
            shape(16, LANES, dtype=jnp.int32),
            shape(512, 512, dtype=BF16),
            shape(256, 1024, dtype=BF16),
            shape(NVAR * ROWS, LANES),
            shape(LINES, 1024, dtype=BF16),
            shape(LINES, 1024, dtype=BF16),
            shape(LINES, LANES),
            shape(LINES, LANES),
        ],
        [HB] * 5,
        [VM] * 9,
        [
            pltpu.VMEM((NVAR * ROWS, LANES), F32),
            pltpu.VMEM((32, LANES), F32),
            pltpu.VMEM((256, LANES), F32),
            pltpu.VMEM((4, LANES), jnp.int32),
            pltpu.VMEM((512, 512), BF16),
            pltpu.VMEM((512, 512), BF16),
            pltpu.VMEM((256, 1024), BF16),
            pltpu.SemaphoreType.DMA((NVAR + 4,)),
        ],
        2_000_000_000,
    )(in_hbm(state), in_hbm(metric), in_hbm(edge_peer), in_hbm(edge_code), in_hbm(work_class))
    from_far = swapped(far, axes, far_partner)
    acc = call(
        second_kernel,
        shape(NVAR * ROWS, LANES),
        [VM] * 5,
        VM,
        [pltpu.VMEM((LINES, 1024), F32)],
        4_000_000_000,
    )(code, acc, high, low, own)
    near, acc = lax.optimization_barrier((near, acc))
    from_near = swapped(near, axes, near_partner)
    mixed1, rain = call(
        third_kernel,
        [shape(3 * ROWS, LANES), shape(8 * CAP, LANES)],
        [SM] + [VM] * 6,
        [VM, VM],
        [
            pltpu.VMEM((LINES, 1024), F32),
            pltpu.VMEM((3 * ROWS, LANES), F32),
            pltpu.VMEM((16, LANES), F32),
            pltpu.SMEM((8,), jnp.int32),
        ],
        2_000_000_000,
    )(owner, code, work, acc, halo, from_near, from_far)
    rain = lax.all_to_all(rain.reshape(8, CAP, LANES), "col", split_axis=0, concat_axis=0, tiled=True)
    new_state = call(
        fourth_kernel,
        shape(NVAR * ROWS, LANES),
        [VM] * 6,
        HB,
        [
            pltpu.VMEM((LINES, 1024), F32),
            pltpu.VMEM((NVAR * ROWS, LANES), F32),
            pltpu.SemaphoreType.DMA((NVAR,)),
        ],
        10_000_000_000,
    )(code, acc, halo, from_near, from_far, mixed1)
    new_state, rain = lax.optimization_barrier((new_state, rain))
    return new_state.reshape(NVAR, LEV, 16, LANES), rain.reshape(1, 1, 8 * CAP, LANES)


def solution(mesh):
    placed = (
        P(None, None, None, ("elem", "col")),
        P(None, None, ("elem", "col")),
        P(None, ("elem", "col")),
        P(None, ("elem", "col")),
        P(("elem", "col"), None),
        P(None, ("elem", "col")),
    )
    return jax.shard_map(
        body,
        mesh=mesh,
        in_specs=placed,
        out_specs=(P(None, None, None, ("elem", "col")), P("elem", "col", None, None)),
        check_vma=False,
    )
```

```python
import jax
import jax.numpy as jnp
import numpy as np
from jax import lax
from jax.experimental import pallas as pl
from jax.experimental.pallas import tpu as pltpu
from jax.sharding import PartitionSpec as P

LEV = 72
GROUPS = LEV // 8
ROWS = LEV * 16
LANES = 128
EDGE_POINTS = ((0, 1, 2, 3), (3, 7, 11, 15), (12, 13, 14, 15), (0, 4, 8, 12))
RIM_POINTS = (0, 1, 2, 3, 4, 7, 8, 11, 12, 13, 14, 15)
CORNERS = (0, 3, 12, 15)
SCALE = 0.5 * 0.03
ORDER = (2, 3, 4, 0, 1, 5, 6)
NVAR = 7
AHEAD = 3
LINES = NVAR * GROUPS * 16
CAP = 3
F32 = jnp.float32
BF16 = jnp.bfloat16
VMEM_LIMIT = 20 * 1024 * 1024


def derivative_matrix():
    nodes = np.array([-1.0, -1.0 / np.sqrt(5.0), 1.0 / np.sqrt(5.0), 1.0])
    weights = np.array(
        [1.0 / np.prod([nodes[a] - nodes[b] for b in range(4) if b != a]) for a in range(4)]
    )
    table = np.zeros((4, 4))
    for a in range(4):
        for b in range(4):
            if a != b:
                table[a, b] = weights[b] / weights[a] / (nodes[a] - nodes[b])
        table[a, a] = -table[a].sum()
    return table


DG = derivative_matrix()
EVEN0 = float((DG[0, 0] + DG[0, 3]) / 2)
EVEN1 = float((DG[1, 0] + DG[1, 3]) / 2)
ODD00 = float((DG[0, 0] - DG[0, 3]) / 2)
ODD01 = float((DG[0, 1] - DG[0, 2]) / 2)
ODD10 = float((DG[1, 0] - DG[1, 3]) / 2)
ODD11 = float((DG[1, 1] - DG[1, 2]) / 2)


def derive_fluxes(u0, u1, u2, u3):
    even = (u0 + u3) - (u1 + u2)
    o0 = u0 - u3
    o1 = u1 - u2
    b0 = (ODD00 / EVEN0) * o0 + (ODD01 / EVEN0) * o1
    b1 = (ODD10 / EVEN1) * o0 + (ODD11 / EVEN1) * o1
    return even + b0, even + b1, b1 - even, b0 - even


def derive_again(u0, u1, u2, u3):
    even = (u0 + u3) - (u1 + u2)
    o0 = u0 - u3
    o1 = u1 - u2
    a1 = (EVEN1 / EVEN0) * even
    b0 = (ODD00 / EVEN0) * o0 + (ODD01 / EVEN0) * o1
    b1 = (ODD10 / EVEN0) * o0 + (ODD11 / EVEN0) * o1
    return even + b0, a1 + b1, b1 - a1, b0 - even


def metric_scale(direction, point):
    row = (point // 4, point % 4)[1 - direction]
    return SCALE * EVEN0 * (EVEN0, EVEN1, EVEN1, EVEN0)[row]


def scaled_tendency(u, metric):
    total = [None] * 16
    for b in range(4):
        points = [4 * b + a for a in range(4)]
        flux = derive_fluxes(*[u[p] for p in points])
        for p, value in zip(points, derive_again(*[f * metric(0, p) for f, p in zip(flux, points)])):
            total[p] = value
    for a in range(4):
        points = [a + 4 * b for b in range(4)]
        flux = derive_fluxes(*[u[p] for p in points])
        for p, value in zip(points, derive_again(*[f * metric(1, p) for f, p in zip(flux, points)])):
            total[p] = total[p] + value
    return total


def edge_rows(peer_ref, code_ref, me, devices):
    rows = []
    for k in range(4):
        peer = peer_ref[k : k + 1, :]
        code = code_ref[k : k + 1, :]
        offset = lax.shift_right_logical(peer, 7) - me
        source = lax.shift_right_logical(code, 1) * LANES + lax.bitwise_and(peer, LANES - 1)
        rows.append(
            dict(
                source=source,
                own=offset == 0,
                after=(offset == 1) | (offset == 1 - devices),
                before=(offset == -1) | (offset == devices - 1),
            )
        )
    return rows


def one_hot(mask):
    return jnp.where(mask, 1.0, 0.0).astype(BF16)


def slots_of(rows, even, hit_ref, less_ref, pack_ref, slots_ref):
    number = lax.broadcasted_iota(jnp.int32, (512, LANES), 0)
    for k, row in enumerate(rows):
        low = slice(k * LANES, (k + 1) * LANES)
        hit_ref[:, low] = one_hot(number == jnp.where(row["before"], row["source"], -1))
        less_ref[:, low] = one_hot(number < row["source"])
    met = lax.dot_general(
        jnp.ones((16, 512), BF16), hit_ref[...], (((1,), (1,)), ((), ())), preferred_element_type=F32
    )
    before_slot = jnp.dot(met.astype(BF16), less_ref[...], preferred_element_type=F32)
    lower = one_hot(
        lax.broadcasted_iota(jnp.int32, (LANES, LANES), 0) < lax.broadcasted_iota(jnp.int32, (LANES, LANES), 1)
    )
    passed = jnp.zeros((1, 1), F32)
    slot = lax.broadcasted_iota(jnp.int32, (64, LANES), 0)
    for k, row in enumerate(rows):
        low = slice(k * LANES, (k + 1) * LANES)
        meets = jnp.where(row["after"], 1.0, 0.0)
        after_slot = passed + jnp.dot(
            jnp.broadcast_to(meets, (16, LANES)).astype(BF16), lower, preferred_element_type=F32
        )
        passed = passed + jnp.sum(meets, axis=1, keepdims=True)
        after = jnp.where(row["after"], after_slot[0:1, :], -1.0).astype(jnp.int32)
        before = jnp.where(row["before"], before_slot[0:1, low], -1.0).astype(jnp.int32)
        near = jnp.where(even, after, before)
        far = jnp.where(even, before, after)
        slots_ref[0:1, low] = near
        slots_ref[1:2, low] = far
        high = slice(512 + k * LANES, 512 + (k + 1) * LANES)
        pack_ref[0:64, low] = pack_ref[64:128, high] = one_hot(slot == near)
        pack_ref[128:192, high] = pack_ref[192:256, low] = one_hot(slot == far)
        pack_ref[0:64, high] = pack_ref[64:128, low] = jnp.zeros((64, LANES), BF16)
        pack_ref[128:192, low] = pack_ref[192:256, high] = jnp.zeros((64, LANES), BF16)

def place_weights(rows, slots_ref, own_ref, halo_ref):
    number = lax.broadcasted_iota(jnp.int32, (512, LANES), 0)
    slot = lax.broadcasted_iota(jnp.int32, (64, LANES), 0)
    for k, row in enumerate(rows):
        low = slice(k * LANES, (k + 1) * LANES)
        high = slice(512 + k * LANES, 512 + (k + 1) * LANES)
        own_ref[:, low] = one_hot(number == jnp.where(row["own"], row["source"], -1))
        near = one_hot(slot == slots_ref[0:1, low])
        far = one_hot(slot == slots_ref[1:2, low])
        for again in (0, 128):
            halo_ref[again : again + 64, low] = near
            halo_ref[again + 64 : again + 128, low] = far
            halo_ref[again : again + 64, high] = far
            halo_ref[again + 64 : again + 128, high] = near


def split(value):
    top = value.astype(BF16)
    return top, (value - top.astype(F32)).astype(BF16)


def edges_out(state_ref, metric_ref, pack_ref, acc_ref, high_ref, low_ref, near_ref, far_refs, ready):
    flat = state_ref.reshape(2 * NVAR * LEV * 8, LANES)

    def metric(direction, point):
        row = 8 * (16 * direction + point)
        return metric_ref[row : row + 8, :]

    def group(index, carry):
        base = index * 64
        u = [
            flat[pl.ds(base + (p // 8) * (NVAR * LEV * 8) + p % 8, 8, stride=8), :] for p in range(16)
        ]
        tendency = scaled_tendency(u, metric)
        for p in range(16):
            if p in CORNERS:
                value = u[p]
            elif p in RIM_POINTS:
                value = u[p] + tendency[p]
            else:
                value = u[p] + 2.0 * tendency[p]
            acc_ref[pl.ds(pl.multiple_of(index * 128 + 8 * p, 8), 8), :] = value
        rows = pl.ds(pl.multiple_of(index * 16, 16), 16)
        for k in range(4):
            for half in range(2):
                first, second = EDGE_POINTS[k][2 * half : 2 * half + 2]
                place = slice(half * 512 + k * LANES, half * 512 + (k + 1) * LANES)
                top, rest = split(jnp.concatenate([tendency[first], tendency[second]], 0))
                high_ref[rows, place] = top
                low_ref[rows, place] = rest
        return carry

    def variable(var, carry):
        ready(var)
        return lax.fori_loop(var * GROUPS, (var + 1) * GROUPS, group, carry)

    lax.fori_loop(0, NVAR, variable, 0)
    across = (((1,), (1,)), ((), ()))
    packed = lax.dot_general(
        high_ref[...], pack_ref[...], across, preferred_element_type=F32
    ) + lax.dot_general(low_ref[...], pack_ref[...], across, preferred_element_type=F32)
    near_ref[...] = packed[:, :LANES]
    far_refs[0][...] = packed[: 3 * 144, LANES:]
    far_refs[1][...] = packed[3 * 144 :, LANES:]


def first_kernel(devices, state_hbm, metric_hbm, peer_hbm, code_hbm, work_hbm,
                 peer_ref, code_ref, work_ref, slots_ref, acc_ref, high_ref, low_ref,
                 near_ref, far0_ref, far1_ref, state_ref, metric_ref, scaled_ref, hit_ref, less_ref, pack_ref, small_sems, sems):
    me = lax.axis_index(("elem", "col"))
    small = [
        pltpu.make_async_copy(source, target, small_sems.at[i])
        for i, (source, target) in enumerate(
            [(peer_hbm, peer_ref), (code_hbm, code_ref), (metric_hbm, metric_ref), (work_hbm, work_ref)]
        )
    ]

    def half_of(i, half):
        var = jnp.where(i < 3, i + 2, jnp.where(i < 5, i - 3, i))
        return pltpu.make_async_copy(
            state_hbm.at[pl.ds(var * LEV, LEV), pl.ds(8 * half, 8), :],
            state_ref.at[half, pl.ds(i * LEV, LEV)],
            sems.at[i, half],
        )

    def fetch(i):
        for half in range(2):
            half_of(i, half).start()

    for copy in small:
        copy.start()
    fetch(0)
    fetch(1)
    small[0].wait()
    small[1].wait()
    rows = edge_rows(peer_ref, code_ref, me, devices)
    slots_of(rows, lax.rem(me, 2) == 0, hit_ref, less_ref, pack_ref, slots_ref)
    small[2].wait()
    small[3].wait()
    for i in range(32):
        scaled_ref[8 * i : 8 * i + 8, :] = jnp.broadcast_to(
            metric_scale(i // 16, i % 16) * metric_ref[i : i + 1, :], (8, LANES)
        )

    def ready(i):
        for half in range(2):
            half_of(i, half).wait()

        @pl.when(i + AHEAD < NVAR)
        def _():
            fetch(i + AHEAD)

    for i in range(2, AHEAD):
        fetch(i)
    edges_out(state_ref, scaled_ref, pack_ref, acc_ref, high_ref, low_ref,
              near_ref, (far0_ref, far1_ref), ready)


def turned_edges(code_ref):
    return [
        jnp.broadcast_to(lax.bitwise_and(code_ref[k : k + 1, :], 1), (8, LANES)) == 1 for k in range(4)
    ]


def averaged(index, line_index, turned, acc_ref, lines_ref):
    base = index * 128
    value = [acc_ref[pl.ds(pl.multiple_of(base + 8 * p, 8), 8), :] for p in range(16)]
    for k in range(4):
        line = []
        for half in range(2):
            place = slice(half * 512 + k * LANES, half * 512 + (k + 1) * LANES)
            for second in range(2):
                rows = pl.ds(pl.multiple_of(line_index * 16 + 8 * second, 8), 8)
                line.append(lines_ref[rows, place])
        for t in range(4):
            p = EDGE_POINTS[k][t]
            value[p] = value[p] + jnp.where(turned[k], line[3 - t], line[t])
    return value


def second_kernel(devices, peer_ref, code_ref, slots_ref, acc_ref, high_ref, low_ref,
                  halo_ref, first_ref, rest_ref, own_ref, lines_ref):
    me = lax.axis_index(("elem", "col"))
    place_weights(edge_rows(peer_ref, code_ref, me, devices), slots_ref, own_ref, halo_ref)

    for half in range(2):
        place = slice(half * 512, (half + 1) * 512)
        lines_ref[:, place] = jnp.dot(
            high_ref[:, place], own_ref[...], preferred_element_type=F32
        ) + jnp.dot(low_ref[:, place], own_ref[...], preferred_element_type=F32)
    turned = turned_edges(code_ref)

    def group_into(out_ref, skipped):
        def group(index, carry):
            for p, value in enumerate(averaged(index, index, turned, acc_ref, lines_ref)):
                out_ref[pl.ds(pl.multiple_of((index - skipped * GROUPS) * 128 + 8 * p, 8), 8), :] = value
            return carry

        return group

    lax.fori_loop(0, 3 * GROUPS, group_into(first_ref, 0), 0)
    lax.fori_loop(3 * GROUPS, NVAR * GROUPS, group_into(rest_ref, 3), 0)


LOG2E = float(np.log2(np.e))


def softplus2(y):
    tail = jnp.exp2(jnp.minimum(y, -y))
    small = tail * (LOG2E - (0.5 * LOG2E) * tail)
    return jnp.maximum(y, 0.0) + jnp.where(tail < 1e-3, small, jnp.log2(1.0 + tail))


UNROLL = 8


def level(half, var, number):
    return pl.ds((half * 3 + var) * (LEV * 8) + number, 8)


def physics(dyn_ref, mark_ref):
    work = [mark_ref[8 * half : 8 * half + 8, :] for half in range(2)]
    marks = [[jnp.where(w >= section, 1.0, 0.0) for section in (1, 2, 3)] for w in work]

    def condense(block, rain):
        base = pl.multiple_of(block * (8 * UNROLL), 8)
        rain = list(rain)
        for step in range(UNROLL):
            for half in range(2):
                heat_at, vapour_at, water_at = [level(half, var, base + 8 * step) for var in range(3)]
                heat = dyn_ref[heat_at, :]
                vapour = dyn_ref[vapour_at, :]
                excess = LOG2E * vapour - (0.5 * LOG2E) * heat
                total = None
                for mark in marks[half]:
                    amount = mark * softplus2(excess)
                    excess = excess - (1.25 * 0.3) * amount
                    total = amount if total is None else total + amount
                total = (0.3 / LOG2E) * total
                dyn_ref[heat_at, :] = heat + 0.5 * total
                dyn_ref[vapour_at, :] = vapour - total
                dyn_ref[water_at, :] = dyn_ref[water_at, :] + total
                rain[half] = rain[half] + total
        return tuple(rain)

    zero = jnp.zeros((8, LANES), F32)
    return jnp.concatenate(lax.fori_loop(0, LEV // UNROLL, condense, (zero, zero)), axis=0)


def mixed(var, dyn_ref, out_ref):
    for half in range(2):

        def at(number, half=half):
            return dyn_ref[level(half, var, 8 * number), :]

        here = at(0)
        above = here + here
        for number in range(LEV):
            lower = at(min(number + 1, LEV - 1))
            below = here + lower
            out_ref[level(half, var, 8 * number), :] = 0.25 * (above + below)
            here, above = lower, below


def by_span(rain):
    point = lax.broadcasted_iota(jnp.int32, (16, LANES), 0)
    eighth = lax.shift_right_logical(lax.broadcasted_iota(jnp.int32, (16, LANES), 1), 3)
    total = None
    for shift in range(16):
        moved = pltpu.roll(rain, 8 * shift, 1) if shift else rain
        kept = jnp.where(point == eighth, moved, 0.0)
        kept = pltpu.roll(kept, 16 - shift, 0) if shift else kept
        total = kept if total is None else total + kept
    return total


def halo_lines(first, near_ref, far_ref, halo_ref, lines_ref):
    rows = slice(first * 144, first * 144 + far_ref.shape[0])
    lane = lax.broadcasted_iota(jnp.int32, far_ref.shape, 1)
    for half in range(2):
        low, high = near_ref[rows, :], far_ref[...]
        if half:
            low, high = high, low
        halo = jnp.concatenate(split(jnp.where(lane < 64, low, high)), axis=1)
        place = slice(half * 512, (half + 1) * 512)
        lines_ref[:, place] = jnp.dot(halo, halo_ref[:, place], preferred_element_type=F32)


def leave(i, source, source_at, state_out, sems):
    return [
        pltpu.make_async_copy(
            source.at[half, pl.ds(source_at * LEV, LEV)],
            state_out.at[pl.ds(ORDER[i] * LEV, LEV), pl.ds(8 * half, 8), :],
            sems.at[2 * i + half],
        )
        for half in range(2)
    ]


def into_halves(index, count, values, flat):
    for p, value in enumerate(values):
        flat[pl.ds(index * 64 + (p // 8) * (count * LEV * 8) + p % 8, 8, stride=8), :] = value


def third_kernel(owner_ref, code_ref, mark_ref, acc_ref, halo_ref, near_ref, far_ref,
                 mixed_ref, rain_ref,
                 lines_ref, dyn_ref, rain_rows, counts):
    halo_lines(0, near_ref, far_ref, halo_ref, lines_ref)
    turned = turned_edges(code_ref)
    flat = dyn_ref.reshape(2 * 3 * LEV * 8, LANES)
    flat_out = mixed_ref.reshape(2 * 3 * LEV * 8, LANES)

    def group(index, carry):
        into_halves(index, 3, averaged(index, index, turned, acc_ref, lines_ref), flat)
        return carry

    lax.fori_loop(0, 3 * GROUPS, group, 0)
    rain = physics(flat, mark_ref)
    for var in range(3):
        mixed(var, flat, flat_out)
    rain_rows[...] = by_span(rain) * (1.0 / LEV)
    rain_ref[...] = jnp.zeros_like(rain_ref)
    for owner in range(8):
        counts[owner] = 0
    for span in range(16):
        owner = owner_ref[span]
        rank = counts[owner]
        counts[owner] = rank + 1
        rain_ref[owner, pl.ds(rank, 1), :] = rain_rows[span : span + 1, :]


def fourth_kernel(code_ref, acc_hbm, halo_ref, near_ref, far_ref, mixed_ref, state_out,
                  lines_ref, acc_ref, dyn_ref, in_sems, sems):
    count = NVAR - 3
    held = [
        pltpu.make_async_copy(
            acc_hbm.at[pl.ds(i * ROWS, ROWS)], acc_ref.at[pl.ds(i * ROWS, ROWS)], in_sems.at[i]
        )
        for i in range(count)
    ]
    for copy in held:
        copy.start()
    halo_lines(3, near_ref, far_ref, halo_ref, lines_ref)
    turned = turned_edges(code_ref)
    flat = dyn_ref.reshape(2 * count * LEV * 8, LANES)

    def group(index, carry):
        into_halves(index, count, averaged(index, index, turned, acc_ref, lines_ref), flat)
        return carry

    copies = sum([leave(i, mixed_ref, i, state_out, sems) for i in range(3)], [])
    for copy in copies:
        copy.start()
    for i in range(count):
        held[i].wait()
        lax.fori_loop(i * GROUPS, (i + 1) * GROUPS, group, 0)
        for copy in leave(i + 3, dyn_ref, i, state_out, sems):
            copy.start()
            copies.append(copy)
    for copy in copies:
        copy.wait()


def swapped(value, axes, partner):
    count = lax.axis_size(axes)
    return lax.ppermute(value, axes, [(source, partner(source, count)) for source in range(count)])


def near_partner(source, count):
    return source + 1 if source % 2 == 0 else source - 1


def far_partner(source, count):
    return (source - 1) % count if source % 2 == 0 else (source + 1) % count


VM = pl.BlockSpec(memory_space=pltpu.VMEM)
SM = pl.BlockSpec(memory_space=pltpu.SMEM)
HB = pl.BlockSpec(memory_space=pltpu.HBM)


def shape(*sizes, dtype=F32):
    return jax.ShapeDtypeStruct(sizes, dtype)


def call(kernel, out, ins, outs, scratch, cost, **more):
    return pl.pallas_call(
        kernel,
        out_shape=out,
        in_specs=ins,
        out_specs=outs,
        scratch_shapes=scratch,
        cost_estimate=pl.CostEstimate(flops=cost, bytes_accessed=cost // 1000, transcendentals=0),
        compiler_params=pltpu.CompilerParams(vmem_limit_bytes=VMEM_LIMIT),
        **more,
    )


def in_hbm(value):
    return pltpu.with_memory_space_constraint(value, pltpu.HBM)


def body(state, metric, edge_peer, edge_code, span_owner, work_class):
    axes = ("elem", "col")
    devices = lax.axis_size(axes)
    state = state.reshape(NVAR * LEV, 16, LANES)
    metric = metric.reshape(32, LANES)
    owner = span_owner.reshape(16)
    count = NVAR - 3
    peer, code, work, slots, acc, high, low, near, far0, far1 = call(
        lambda *refs: first_kernel(devices, *refs),
        [
            shape(4, LANES, dtype=jnp.int32),
            shape(4, LANES, dtype=jnp.int32),
            shape(16, LANES, dtype=jnp.int32),
            shape(8, 512, dtype=jnp.int32),
            shape(NVAR * ROWS, LANES),
            shape(LINES, 1024, dtype=BF16),
            shape(LINES, 1024, dtype=BF16),
            shape(LINES, LANES),
            shape(3 * 144, LANES),
            shape(count * 144, LANES),
        ],
        [HB] * 5,
        [VM] * 10,
        [
            pltpu.VMEM((2, NVAR * LEV, 8, LANES), F32),
            pltpu.VMEM((32, LANES), F32),
            pltpu.VMEM((256, LANES), F32),
            pltpu.VMEM((512, 512), BF16),
            pltpu.VMEM((512, 512), BF16),
            pltpu.VMEM((256, 1024), BF16),
            pltpu.SemaphoreType.DMA((4,)),
            pltpu.SemaphoreType.DMA((NVAR, 2)),
        ],
        2_000_000_000,
    )(in_hbm(state), in_hbm(metric), in_hbm(edge_peer), in_hbm(edge_code), in_hbm(work_class))
    from_far0 = swapped(far0, axes, far_partner)
    from_near = swapped(near, axes, near_partner)
    from_far1 = swapped(far1, axes, far_partner)
    halo, acc, acc_rest = call(
        lambda *refs: second_kernel(devices, *refs),
        [shape(256, 1024, dtype=BF16), shape(3 * ROWS, LANES), shape(count * ROWS, LANES)],
        [VM] * 6,
        [VM] * 3,
        [
            pltpu.VMEM((512, 512), BF16),
            pltpu.VMEM((LINES, 1024), F32),
        ],
        4_000_000_000,
    )(peer, code, slots, acc, high, low)
    mixed1, rain = call(
        third_kernel,
        [shape(2, 3 * LEV, 8, LANES), shape(8, CAP, LANES)],
        [SM] + [VM] * 6,
        [VM, VM],
        [
            pltpu.VMEM((3 * 144, 1024), F32),
            pltpu.VMEM((2, 3 * LEV, 8, LANES), F32),
            pltpu.VMEM((16, LANES), F32),
            pltpu.SMEM((8,), jnp.int32),
        ],
        2_000_000_000,
    )(owner, code, work, acc, halo, from_near, from_far0)
    rain = lax.all_to_all(rain, "col", split_axis=0, concat_axis=0, tiled=True)
    new_state = call(
        fourth_kernel,
        shape(NVAR * LEV, 16, LANES),
        [VM, HB] + [VM] * 4,
        HB,
        [
            pltpu.VMEM((count * 144, 1024), F32),
            pltpu.VMEM((count * ROWS, LANES), F32),
            pltpu.VMEM((2, count * LEV, 8, LANES), F32),
            pltpu.SemaphoreType.DMA((count,)),
            pltpu.SemaphoreType.DMA((2 * NVAR,)),
        ],
        10_000_000_000,
    )(code, in_hbm(acc_rest), halo, from_near, from_far1, mixed1)
    new_state, rain = lax.optimization_barrier((new_state, rain))
    return new_state.reshape(NVAR, LEV, 16, LANES), rain.reshape(1, 1, 8 * CAP, LANES)


def solution(mesh):
    placed = (
        P(None, None, None, ("elem", "col")),
        P(None, None, ("elem", "col")),
        P(None, ("elem", "col")),
        P(None, ("elem", "col")),
        P(("elem", "col"), None),
        P(None, ("elem", "col")),
    )
    return jax.shard_map(
        body,
        mesh=mesh,
        in_specs=placed,
        out_specs=(P(None, None, None, ("elem", "col")), P("elem", "col", None, None)),
        check_vma=False,
    )
```

```python
import jax
import jax.numpy as jnp
import numpy as np
from jax import lax
from jax.experimental import pallas as pl
from jax.experimental.pallas import tpu as pltpu
from jax.sharding import PartitionSpec as P

LEV = 72
GROUPS = LEV // 8
ROWS = LEV * 16
LANES = 128
EDGE_POINTS = ((0, 1, 2, 3), (3, 7, 11, 15), (12, 13, 14, 15), (0, 4, 8, 12))
RIM_POINTS = (0, 1, 2, 3, 4, 7, 8, 11, 12, 13, 14, 15)
CORNERS = (0, 3, 12, 15)
SCALE = 0.5 * 0.03
ORDER = (2, 3, 4, 0, 1, 5, 6)
NVAR = 7
AHEAD = 3
LINES = NVAR * GROUPS * 16
CAP = 3
F32 = jnp.float32
BF16 = jnp.bfloat16
VMEM_LIMIT = 20 * 1024 * 1024


def derivative_matrix():
    nodes = np.array([-1.0, -1.0 / np.sqrt(5.0), 1.0 / np.sqrt(5.0), 1.0])
    weights = np.array(
        [1.0 / np.prod([nodes[a] - nodes[b] for b in range(4) if b != a]) for a in range(4)]
    )
    table = np.zeros((4, 4))
    for a in range(4):
        for b in range(4):
            if a != b:
                table[a, b] = weights[b] / weights[a] / (nodes[a] - nodes[b])
        table[a, a] = -table[a].sum()
    return table


DG = derivative_matrix()
EVEN0 = float((DG[0, 0] + DG[0, 3]) / 2)
EVEN1 = float((DG[1, 0] + DG[1, 3]) / 2)
ODD00 = float((DG[0, 0] - DG[0, 3]) / 2)
ODD01 = float((DG[0, 1] - DG[0, 2]) / 2)
ODD10 = float((DG[1, 0] - DG[1, 3]) / 2)
ODD11 = float((DG[1, 1] - DG[1, 2]) / 2)


def derive_fluxes(u0, u1, u2, u3):
    even = (u0 + u3) - (u1 + u2)
    o0 = u0 - u3
    o1 = u1 - u2
    b0 = (ODD00 / EVEN0) * o0 + (ODD01 / EVEN0) * o1
    b1 = (ODD10 / EVEN1) * o0 + (ODD11 / EVEN1) * o1
    return even + b0, even + b1, b1 - even, b0 - even


def derive_again(u0, u1, u2, u3):
    even = (u0 + u3) - (u1 + u2)
    o0 = u0 - u3
    o1 = u1 - u2
    a1 = (EVEN1 / EVEN0) * even
    b0 = (ODD00 / EVEN0) * o0 + (ODD01 / EVEN0) * o1
    b1 = (ODD10 / EVEN0) * o0 + (ODD11 / EVEN0) * o1
    return even + b0, a1 + b1, b1 - a1, b0 - even


def metric_scale(direction, point):
    row = (point // 4, point % 4)[1 - direction]
    return SCALE * EVEN0 * (EVEN0, EVEN1, EVEN1, EVEN0)[row]


def scaled_tendency(u, metric):
    total = [None] * 16
    for b in range(4):
        points = [4 * b + a for a in range(4)]
        flux = derive_fluxes(*[u[p] for p in points])
        for p, value in zip(points, derive_again(*[f * metric(0, p) for f, p in zip(flux, points)])):
            total[p] = value
    for a in range(4):
        points = [a + 4 * b for b in range(4)]
        flux = derive_fluxes(*[u[p] for p in points])
        for p, value in zip(points, derive_again(*[f * metric(1, p) for f, p in zip(flux, points)])):
            total[p] = total[p] + value
    return total


def edge_rows(peer_ref, code_ref, me, devices):
    rows = []
    for k in range(4):
        peer = peer_ref[k : k + 1, :]
        code = code_ref[k : k + 1, :]
        offset = lax.shift_right_logical(peer, 7) - me
        source = lax.shift_right_logical(code, 1) * LANES + lax.bitwise_and(peer, LANES - 1)
        rows.append(
            dict(
                source=source,
                own=offset == 0,
                after=(offset == 1) | (offset == 1 - devices),
                before=(offset == -1) | (offset == devices - 1),
            )
        )
    return rows


def one_hot(mask):
    return jnp.where(mask, 1.0, 0.0).astype(BF16)


def slots_of(rows, even, hit_ref, less_ref, pack_ref, slots_ref):
    number = lax.broadcasted_iota(jnp.int32, (512, LANES), 0)
    for k, row in enumerate(rows):
        low = slice(k * LANES, (k + 1) * LANES)
        hit_ref[:, low] = one_hot(number == jnp.where(row["before"], row["source"], -1))
        less_ref[:, low] = one_hot(number < row["source"])
    met = lax.dot_general(
        jnp.ones((16, 512), BF16), hit_ref[...], (((1,), (1,)), ((), ())), preferred_element_type=F32
    )
    before_slot = jnp.dot(met.astype(BF16), less_ref[...], preferred_element_type=F32)
    lower = one_hot(
        lax.broadcasted_iota(jnp.int32, (LANES, LANES), 0) < lax.broadcasted_iota(jnp.int32, (LANES, LANES), 1)
    )
    passed = jnp.zeros((1, 1), F32)
    slot = lax.broadcasted_iota(jnp.int32, (64, LANES), 0)
    for k, row in enumerate(rows):
        low = slice(k * LANES, (k + 1) * LANES)
        meets = jnp.where(row["after"], 1.0, 0.0)
        after_slot = passed + jnp.dot(
            jnp.broadcast_to(meets, (16, LANES)).astype(BF16), lower, preferred_element_type=F32
        )
        passed = passed + jnp.sum(meets, axis=1, keepdims=True)
        after = jnp.where(row["after"], after_slot[0:1, :], -1.0).astype(jnp.int32)
        before = jnp.where(row["before"], before_slot[0:1, low], -1.0).astype(jnp.int32)
        near = jnp.where(even, after, before)
        far = jnp.where(even, before, after)
        slots_ref[0:1, low] = near
        slots_ref[1:2, low] = far
        high = slice(512 + k * LANES, 512 + (k + 1) * LANES)
        pack_ref[0:64, low] = pack_ref[64:128, high] = one_hot(slot == near)
        pack_ref[128:192, high] = pack_ref[192:256, low] = one_hot(slot == far)
        pack_ref[0:64, high] = pack_ref[64:128, low] = jnp.zeros((64, LANES), BF16)
        pack_ref[128:192, low] = pack_ref[192:256, high] = jnp.zeros((64, LANES), BF16)

def place_weights(rows, slots_ref, own_ref, halo_ref):
    number = lax.broadcasted_iota(jnp.int32, (512, LANES), 0)
    slot = lax.broadcasted_iota(jnp.int32, (64, LANES), 0)
    for k, row in enumerate(rows):
        low = slice(k * LANES, (k + 1) * LANES)
        high = slice(512 + k * LANES, 512 + (k + 1) * LANES)
        own_ref[:, low] = one_hot(number == jnp.where(row["own"], row["source"], -1))
        near = one_hot(slot == slots_ref[0:1, low])
        far = one_hot(slot == slots_ref[1:2, low])
        for again in (0, 128):
            halo_ref[again : again + 64, low] = near
            halo_ref[again + 64 : again + 128, low] = far
            halo_ref[again : again + 64, high] = far
            halo_ref[again + 64 : again + 128, high] = near


def split(value):
    top = value.astype(BF16)
    return top, (value - top.astype(F32)).astype(BF16)


def edges_out(state_ref, metric_ref, pack_ref, acc_ref, high_ref, low_ref, near_ref, far_refs, ready):
    flat = state_ref.reshape(2 * NVAR * LEV * 8, LANES)

    def metric(direction, point):
        row = 8 * (16 * direction + point)
        return metric_ref[row : row + 8, :]

    def group(index, carry):
        base = index * 64
        u = [
            flat[pl.ds(base + (p // 8) * (NVAR * LEV * 8) + p % 8, 8, stride=8), :] for p in range(16)
        ]
        tendency = scaled_tendency(u, metric)
        for p in range(16):
            if p in CORNERS:
                value = u[p]
            elif p in RIM_POINTS:
                value = u[p] + tendency[p]
            else:
                value = u[p] + 2.0 * tendency[p]
            acc_ref[pl.ds(pl.multiple_of(index * 128 + 8 * p, 8), 8), :] = value
        rows = pl.ds(pl.multiple_of(index * 16, 16), 16)
        for k in range(4):
            for half in range(2):
                first, second = EDGE_POINTS[k][2 * half : 2 * half + 2]
                place = slice(half * 512 + k * LANES, half * 512 + (k + 1) * LANES)
                top, rest = split(jnp.concatenate([tendency[first], tendency[second]], 0))
                high_ref[rows, place] = top
                low_ref[rows, place] = rest
        return carry

    def variable(var, carry):
        ready(var)
        return lax.fori_loop(var * GROUPS, (var + 1) * GROUPS, group, carry)

    lax.fori_loop(0, NVAR, variable, 0)
    across = (((1,), (1,)), ((), ()))
    packed = lax.dot_general(
        high_ref[...], pack_ref[...], across, preferred_element_type=F32
    ) + lax.dot_general(low_ref[...], pack_ref[...], across, preferred_element_type=F32)
    near_ref[...] = packed[:, :LANES]
    far_refs[0][...] = packed[: 3 * 144, LANES:]
    far_refs[1][...] = packed[3 * 144 :, LANES:]


def first_kernel(devices, state_hbm, metric_hbm, peer_hbm, code_hbm, work_hbm,
                 peer_ref, code_ref, work_ref, slots_ref, acc_ref, high_ref, low_ref,
                 near_ref, far0_ref, far1_ref, state_ref, metric_ref, scaled_ref, hit_ref, less_ref, pack_ref, small_sems, sems):
    me = lax.axis_index(("elem", "col"))
    small = [
        pltpu.make_async_copy(source, target, small_sems.at[i])
        for i, (source, target) in enumerate(
            [(peer_hbm, peer_ref), (code_hbm, code_ref), (metric_hbm, metric_ref), (work_hbm, work_ref)]
        )
    ]

    def half_of(i, half):
        var = jnp.where(i < 3, i + 2, jnp.where(i < 5, i - 3, i))
        return pltpu.make_async_copy(
            state_hbm.at[pl.ds(var * LEV, LEV), pl.ds(8 * half, 8), :],
            state_ref.at[half, pl.ds(i * LEV, LEV)],
            sems.at[i, half],
        )

    def fetch(i):
        for half in range(2):
            half_of(i, half).start()

    for copy in small:
        copy.start()
    fetch(0)
    fetch(1)
    small[0].wait()
    small[1].wait()
    rows = edge_rows(peer_ref, code_ref, me, devices)
    slots_of(rows, lax.rem(me, 2) == 0, hit_ref, less_ref, pack_ref, slots_ref)
    small[2].wait()
    small[3].wait()
    for i in range(32):
        scaled_ref[8 * i : 8 * i + 8, :] = jnp.broadcast_to(
            metric_scale(i // 16, i % 16) * metric_ref[i : i + 1, :], (8, LANES)
        )

    def ready(i):
        for half in range(2):
            half_of(i, half).wait()

        @pl.when(i + AHEAD < NVAR)
        def _():
            fetch(i + AHEAD)

    for i in range(2, AHEAD):
        fetch(i)
    edges_out(state_ref, scaled_ref, pack_ref, acc_ref, high_ref, low_ref,
              near_ref, (far0_ref, far1_ref), ready)


def turned_edges(code_ref):
    return [
        jnp.broadcast_to(lax.bitwise_and(code_ref[k : k + 1, :], 1), (8, LANES)) == 1 for k in range(4)
    ]


def averaged(index, line_index, turned, acc_ref, lines_ref):
    base = index * 128
    value = [acc_ref[pl.ds(pl.multiple_of(base + 8 * p, 8), 8), :] for p in range(16)]
    for k in range(4):
        line = []
        for half in range(2):
            place = slice(half * 512 + k * LANES, half * 512 + (k + 1) * LANES)
            for second in range(2):
                rows = pl.ds(pl.multiple_of(line_index * 16 + 8 * second, 8), 8)
                line.append(lines_ref[rows, place])
        for t in range(4):
            p = EDGE_POINTS[k][t]
            value[p] = value[p] + jnp.where(turned[k], line[3 - t], line[t])
    return value


def own_lines(first, count, high_ref, low_ref, own_ref, half):
    rows = slice(first * 144, (first + count) * 144)
    place = slice(half * 512, (half + 1) * 512)
    return jnp.dot(high_ref[rows, place], own_ref[...], preferred_element_type=F32) + jnp.dot(
        low_ref[rows, place], own_ref[...], preferred_element_type=F32
    )


def second_kernel(devices, peer_ref, code_ref, slots_ref, acc_ref, high_ref, low_ref,
                  own_ref, halo_ref, first_ref, lines_ref):
    me = lax.axis_index(("elem", "col"))
    place_weights(edge_rows(peer_ref, code_ref, me, devices), slots_ref, own_ref, halo_ref)
    for half in range(2):
        lines_ref[:, half * 512 : (half + 1) * 512] = own_lines(0, 3, high_ref, low_ref, own_ref, half)
    turned = turned_edges(code_ref)

    def group(index, carry):
        for p, value in enumerate(averaged(index, index, turned, acc_ref, lines_ref)):
            first_ref[pl.ds(pl.multiple_of(index * 128 + 8 * p, 8), 8), :] = value
        return carry

    lax.fori_loop(0, 3 * GROUPS, group, 0)


LOG2E = float(np.log2(np.e))


def softplus2(y):
    tail = jnp.exp2(jnp.minimum(y, -y))
    small = tail * (LOG2E - (0.5 * LOG2E) * tail)
    return jnp.maximum(y, 0.0) + jnp.where(tail < 1e-3, small, jnp.log2(1.0 + tail))


UNROLL = 8


def level(half, var, number):
    return pl.ds((half * 3 + var) * (LEV * 8) + number, 8)


def physics(dyn_ref, mark_ref):
    work = [mark_ref[8 * half : 8 * half + 8, :] for half in range(2)]
    marks = [[jnp.where(w >= section, 1.0, 0.0) for section in (1, 2, 3)] for w in work]

    def condense(block, rain):
        base = pl.multiple_of(block * (8 * UNROLL), 8)
        rain = list(rain)
        for step in range(UNROLL):
            for half in range(2):
                heat_at, vapour_at, water_at = [level(half, var, base + 8 * step) for var in range(3)]
                heat = dyn_ref[heat_at, :]
                vapour = dyn_ref[vapour_at, :]
                excess = LOG2E * vapour - (0.5 * LOG2E) * heat
                total = None
                for mark in marks[half]:
                    amount = mark * softplus2(excess)
                    excess = excess - (1.25 * 0.3) * amount
                    total = amount if total is None else total + amount
                total = (0.3 / LOG2E) * total
                dyn_ref[heat_at, :] = heat + 0.5 * total
                dyn_ref[vapour_at, :] = vapour - total
                dyn_ref[water_at, :] = dyn_ref[water_at, :] + total
                rain[half] = rain[half] + total
        return tuple(rain)

    zero = jnp.zeros((8, LANES), F32)
    return jnp.concatenate(lax.fori_loop(0, LEV // UNROLL, condense, (zero, zero)), axis=0)


def mixed(var, dyn_ref, out_ref):
    for half in range(2):

        def at(number, half=half):
            return dyn_ref[level(half, var, 8 * number), :]

        here = at(0)
        above = here + here
        for number in range(LEV):
            lower = at(min(number + 1, LEV - 1))
            below = here + lower
            out_ref[level(half, var, 8 * number), :] = 0.25 * (above + below)
            here, above = lower, below


def by_span(rain):
    point = lax.broadcasted_iota(jnp.int32, (16, LANES), 0)
    eighth = lax.shift_right_logical(lax.broadcasted_iota(jnp.int32, (16, LANES), 1), 3)
    total = None
    for shift in range(16):
        moved = pltpu.roll(rain, 8 * shift, 1) if shift else rain
        kept = jnp.where(point == eighth, moved, 0.0)
        kept = pltpu.roll(kept, 16 - shift, 0) if shift else kept
        total = kept if total is None else total + kept
    return total


def halo_lines(first, near_ref, far_ref, halo_ref, half):
    rows = slice(first * 144, first * 144 + far_ref.shape[0])
    lane = lax.broadcasted_iota(jnp.int32, far_ref.shape, 1)
    low, high = near_ref[rows, :], far_ref[...]
    if half:
        low, high = high, low
    halo = jnp.concatenate(split(jnp.where(lane < 64, low, high)), axis=1)
    return jnp.dot(halo, halo_ref[:, half * 512 : (half + 1) * 512], preferred_element_type=F32)


def leave(i, source, source_at, state_out, sems):
    return [
        pltpu.make_async_copy(
            source.at[half, pl.ds(source_at * LEV, LEV)],
            state_out.at[pl.ds(ORDER[i] * LEV, LEV), pl.ds(8 * half, 8), :],
            sems.at[2 * i + half],
        )
        for half in range(2)
    ]


def into_halves(index, count, values, flat):
    for p, value in enumerate(values):
        flat[pl.ds(index * 64 + (p // 8) * (count * LEV * 8) + p % 8, 8, stride=8), :] = value


def third_kernel(owner_ref, code_ref, mark_ref, acc_ref, halo_ref, near_ref, far_ref,
                 mixed_ref, keep_ref, send_ref,
                 lines_ref, dyn_ref, rain_rows, counts):
    me = lax.axis_index("col")
    for half in range(2):
        lines_ref[:, half * 512 : (half + 1) * 512] = halo_lines(0, near_ref, far_ref, halo_ref, half)
    turned = turned_edges(code_ref)
    flat = dyn_ref.reshape(2 * 3 * LEV * 8, LANES)
    flat_out = mixed_ref.reshape(2 * 3 * LEV * 8, LANES)

    def group(index, carry):
        into_halves(index, 3, averaged(index, index, turned, acc_ref, lines_ref), flat)
        return carry

    lax.fori_loop(0, 3 * GROUPS, group, 0)
    rain = physics(flat, mark_ref)
    for var in range(3):
        mixed(var, flat, flat_out)
    rain_rows[...] = by_span(rain) * (1.0 / LEV)
    keep_ref[...] = jnp.zeros_like(keep_ref)
    send_ref[...] = jnp.zeros_like(send_ref)
    for owner in range(8):
        counts[owner] = 0
    for span in range(16):
        owner = owner_ref[span]
        rank = counts[owner]
        counts[owner] = rank + 1
        way = lax.bitwise_xor(owner, me)
        place = 8 * (way // 2 % 2) + 4 * (way // 4) + rank

        @pl.when(way % 2 == 0)
        def _(place=place, span=span):
            keep_ref[pl.ds(place, 1), :] = rain_rows[span : span + 1, :]

        @pl.when(way % 2 == 1)
        def _(place=place, span=span):
            send_ref[pl.ds(place, 1), :] = rain_rows[span : span + 1, :]


def fourth_kernel(code_ref, acc_ref, high_ref, low_ref, own_ref, halo_ref, near_ref, far_ref,
                  dyn_ref, lines_ref):
    count = NVAR - 3
    for half in range(2):
        lines_ref[:, half * 512 : (half + 1) * 512] = own_lines(
            3, count, high_ref, low_ref, own_ref, half
        ) + halo_lines(3, near_ref, far_ref, halo_ref, half)
    turned = turned_edges(code_ref)
    flat = dyn_ref.reshape(2 * count * LEV * 8, LANES)

    def group(index, carry):
        into_halves(index, count, averaged(index + 3 * GROUPS, index, turned, acc_ref, lines_ref), flat)
        return carry

    lax.fori_loop(0, count * GROUPS, group, 0)


def fifth_kernel(mixed_ref, dyn_ref, state_out, sems):
    copies = sum([leave(i, mixed_ref, i, state_out, sems) for i in range(3)], [])
    copies += sum([leave(i + 3, dyn_ref, i, state_out, sems) for i in range(NVAR - 3)], [])
    for copy in copies:
        copy.start()
    for copy in copies:
        copy.wait()


def sixth_kernel(keep_ref, first_ref, second_ref, third_ref, rain_ref):
    me = lax.axis_index("col")
    found = [keep_ref[0:4, :], first_ref[0:4, :], second_ref[0:4, :], second_ref[8:12, :]]
    found += [third_ref[4 * i : 4 * i + 4, :] for i in range(4)]
    for way, rows in enumerate(found):
        for rank in range(CAP):
            rain_ref[pl.ds(CAP * lax.bitwise_xor(me, way) + rank, 1), :] = rows[rank : rank + 1, :]


def swapped(value, axes, partner):
    count = lax.axis_size(axes)
    return lax.ppermute(value, axes, [(source, partner(source, count)) for source in range(count)])


def near_partner(source, count):
    return source + 1 if source % 2 == 0 else source - 1


def far_partner(source, count):
    return (source - 1) % count if source % 2 == 0 else (source + 1) % count


VM = pl.BlockSpec(memory_space=pltpu.VMEM)
SM = pl.BlockSpec(memory_space=pltpu.SMEM)
HB = pl.BlockSpec(memory_space=pltpu.HBM)


def shape(*sizes, dtype=F32):
    return jax.ShapeDtypeStruct(sizes, dtype)


def call(kernel, out, ins, outs, scratch, cost, **more):
    return pl.pallas_call(
        kernel,
        out_shape=out,
        in_specs=ins,
        out_specs=outs,
        scratch_shapes=scratch,
        cost_estimate=pl.CostEstimate(flops=cost, bytes_accessed=cost // 1000, transcendentals=0),
        compiler_params=pltpu.CompilerParams(vmem_limit_bytes=VMEM_LIMIT),
        **more,
    )


def in_hbm(value):
    return pltpu.with_memory_space_constraint(value, pltpu.HBM)


def body(state, metric, edge_peer, edge_code, span_owner, work_class):
    axes = ("elem", "col")
    devices = lax.axis_size(axes)
    state = state.reshape(NVAR * LEV, 16, LANES)
    metric = metric.reshape(32, LANES)
    owner = span_owner.reshape(16)
    count = NVAR - 3
    peer, code, work, slots, acc, high, low, near, far0, far1 = call(
        lambda *refs: first_kernel(devices, *refs),
        [
            shape(4, LANES, dtype=jnp.int32),
            shape(4, LANES, dtype=jnp.int32),
            shape(16, LANES, dtype=jnp.int32),
            shape(8, 512, dtype=jnp.int32),
            shape(NVAR * ROWS, LANES),
            shape(LINES, 1024, dtype=BF16),
            shape(LINES, 1024, dtype=BF16),
            shape(LINES, LANES),
            shape(3 * 144, LANES),
            shape(count * 144, LANES),
        ],
        [HB] * 5,
        [VM] * 10,
        [
            pltpu.VMEM((2, NVAR * LEV, 8, LANES), F32),
            pltpu.VMEM((32, LANES), F32),
            pltpu.VMEM((256, LANES), F32),
            pltpu.VMEM((512, 512), BF16),
            pltpu.VMEM((512, 512), BF16),
            pltpu.VMEM((256, 1024), BF16),
            pltpu.SemaphoreType.DMA((4,)),
            pltpu.SemaphoreType.DMA((NVAR, 2)),
        ],
        2_000_000_000,
    )(in_hbm(state), in_hbm(metric), in_hbm(edge_peer), in_hbm(edge_code), in_hbm(work_class))
    from_far0 = swapped(far0, axes, far_partner)
    from_near = swapped(near, axes, near_partner)
    from_far1 = swapped(far1, axes, far_partner)
    own, halo, first = call(
        lambda *refs: second_kernel(devices, *refs),
        [shape(512, 512, dtype=BF16), shape(256, 1024, dtype=BF16), shape(3 * ROWS, LANES)],
        [VM] * 6,
        [VM] * 3,
        [pltpu.VMEM((3 * 144, 1024), F32)],
        2_000_000_000,
    )(peer, code, slots, acc, high, low)
    mixed1, keep, send = call(
        third_kernel,
        [shape(2, 3 * LEV, 8, LANES), shape(16, LANES), shape(16, LANES)],
        [SM] + [VM] * 6,
        [VM] * 3,
        [
            pltpu.VMEM((3 * 144, 1024), F32),
            pltpu.VMEM((2, 3 * LEV, 8, LANES), F32),
            pltpu.VMEM((16, LANES), F32),
            pltpu.SMEM((8,), jnp.int32),
        ],
        2_000_000_000,
    )(owner, code, work, first, halo, from_near, from_far0)
    rain1 = swapped(send, "col", lambda source, size: source ^ 1)
    dyn = call(
        fourth_kernel,
        shape(2, count * LEV, 8, LANES),
        [VM] * 8,
        VM,
        [pltpu.VMEM((count * 144, 1024), F32)],
        4_000_000_000,
    )(code, acc, high, low, own, halo, from_near, from_far1)
    keep, rain1, dyn = lax.optimization_barrier((keep, rain1, dyn))
    send = jnp.concatenate([keep[8:16], rain1[8:16]], axis=0)
    rain2 = swapped(send, "col", lambda source, size: source ^ 2)
    new_state = call(
        fifth_kernel,
        shape(NVAR * LEV, 16, LANES),
        [VM, VM],
        HB,
        [pltpu.SemaphoreType.DMA((2 * NVAR,))],
        4_000_000_000,
    )(mixed1, dyn)
    keep, rain1, rain2, new_state = lax.optimization_barrier((keep, rain1, rain2, new_state))
    send = jnp.concatenate([keep[4:8], rain1[4:8], rain2[4:8], rain2[12:16]], axis=0)
    rain3 = swapped(send, "col", lambda source, size: source ^ 4)
    rain = call(sixth_kernel, shape(8 * CAP, LANES), [VM] * 4, VM, [], 1_000_000)(keep, rain1, rain2, rain3)
    return new_state.reshape(NVAR, LEV, 16, LANES), rain.reshape(1, 1, 8 * CAP, LANES)


def solution(mesh):
    placed = (
        P(None, None, None, ("elem", "col")),
        P(None, None, ("elem", "col")),
        P(None, ("elem", "col")),
        P(None, ("elem", "col")),
        P(("elem", "col"), None),
        P(None, ("elem", "col")),
    )
    return jax.shard_map(
        body,
        mesh=mesh,
        in_specs=placed,
        out_specs=(P(None, None, None, ("elem", "col")), P("elem", "col", None, None)),
        check_vma=False,
    )
```

```python
import jax
import jax.numpy as jnp
import numpy as np
from jax import lax
from jax.experimental import pallas as pl
from jax.experimental.pallas import tpu as pltpu
from jax.sharding import PartitionSpec as P

LEV = 72
GROUPS = LEV // 8
ROWS = LEV * 16
LANES = 128
EDGE_POINTS = ((0, 1, 2, 3), (3, 7, 11, 15), (12, 13, 14, 15), (0, 4, 8, 12))
RIM_POINTS = (0, 1, 2, 3, 4, 7, 8, 11, 12, 13, 14, 15)
CORNERS = (0, 3, 12, 15)
SCALE = 0.5 * 0.03
ORDER = (2, 3, 4, 0, 1, 5, 6)
NVAR = 7
AHEAD = 2
LINES = NVAR * GROUPS * 16
CAP = 3
F32 = jnp.float32
BF16 = jnp.bfloat16
VMEM_LIMIT = 20 * 1024 * 1024


def derivative_matrix():
    nodes = np.array([-1.0, -1.0 / np.sqrt(5.0), 1.0 / np.sqrt(5.0), 1.0])
    weights = np.array(
        [1.0 / np.prod([nodes[a] - nodes[b] for b in range(4) if b != a]) for a in range(4)]
    )
    table = np.zeros((4, 4))
    for a in range(4):
        for b in range(4):
            if a != b:
                table[a, b] = weights[b] / weights[a] / (nodes[a] - nodes[b])
        table[a, a] = -table[a].sum()
    return table


DG = derivative_matrix()
EVEN0 = float((DG[0, 0] + DG[0, 3]) / 2)
EVEN1 = float((DG[1, 0] + DG[1, 3]) / 2)
ODD00 = float((DG[0, 0] - DG[0, 3]) / 2)
ODD01 = float((DG[0, 1] - DG[0, 2]) / 2)
ODD10 = float((DG[1, 0] - DG[1, 3]) / 2)
ODD11 = float((DG[1, 1] - DG[1, 2]) / 2)


def derive_fluxes(u0, u1, u2, u3):
    even = (u0 + u3) - (u1 + u2)
    o0 = u0 - u3
    o1 = u1 - u2
    b0 = (ODD00 / EVEN0) * o0 + (ODD01 / EVEN0) * o1
    b1 = (ODD10 / EVEN1) * o0 + (ODD11 / EVEN1) * o1
    return even + b0, even + b1, b1 - even, b0 - even


def derive_again(u0, u1, u2, u3):
    even = (u0 + u3) - (u1 + u2)
    o0 = u0 - u3
    o1 = u1 - u2
    a1 = (EVEN1 / EVEN0) * even
    b0 = (ODD00 / EVEN0) * o0 + (ODD01 / EVEN0) * o1
    b1 = (ODD10 / EVEN0) * o0 + (ODD11 / EVEN0) * o1
    return even + b0, a1 + b1, b1 - a1, b0 - even


def metric_scale(direction, point):
    row = (point // 4, point % 4)[1 - direction]
    return SCALE * EVEN0 * (EVEN0, EVEN1, EVEN1, EVEN0)[row]


def scaled_tendency(u, metric):
    total = [None] * 16
    for b in range(4):
        points = [4 * b + a for a in range(4)]
        flux = derive_fluxes(*[u[p] for p in points])
        for p, value in zip(points, derive_again(*[f * metric(0, p) for f, p in zip(flux, points)])):
            total[p] = value
    for a in range(4):
        points = [a + 4 * b for b in range(4)]
        flux = derive_fluxes(*[u[p] for p in points])
        for p, value in zip(points, derive_again(*[f * metric(1, p) for f, p in zip(flux, points)])):
            total[p] = total[p] + value
    return total


def edge_rows(peer_ref, code_ref, me, devices):
    rows = []
    for k in range(4):
        peer = peer_ref[k : k + 1, :]
        code = code_ref[k : k + 1, :]
        offset = lax.shift_right_logical(peer, 7) - me
        source = lax.shift_right_logical(code, 1) * LANES + lax.bitwise_and(peer, LANES - 1)
        rows.append(
            dict(
                source=source,
                own=offset == 0,
                after=(offset == 1) | (offset == 1 - devices),
                before=(offset == -1) | (offset == devices - 1),
            )
        )
    return rows


def one_hot(mask):
    return jnp.where(mask, 1.0, 0.0).astype(BF16)


def slots_of(rows, even, hit_ref, less_ref, pack_ref, slots_ref):
    number = lax.broadcasted_iota(jnp.int32, (512, LANES), 0)
    for k, row in enumerate(rows):
        low = slice(k * LANES, (k + 1) * LANES)
        hit_ref[:, low] = one_hot(number == jnp.where(row["before"], row["source"], -1))
        less_ref[:, low] = one_hot(number < row["source"])
    met = lax.dot_general(
        jnp.ones((16, 512), BF16), hit_ref[...], (((1,), (1,)), ((), ())), preferred_element_type=F32
    )
    before_slot = jnp.dot(met.astype(BF16), less_ref[...], preferred_element_type=F32)
    lower = one_hot(
        lax.broadcasted_iota(jnp.int32, (LANES, LANES), 0) < lax.broadcasted_iota(jnp.int32, (LANES, LANES), 1)
    )
    passed = jnp.zeros((1, 1), F32)
    slot = lax.broadcasted_iota(jnp.int32, (64, LANES), 0)
    for k, row in enumerate(rows):
        low = slice(k * LANES, (k + 1) * LANES)
        meets = jnp.where(row["after"], 1.0, 0.0)
        after_slot = passed + jnp.dot(
            jnp.broadcast_to(meets, (16, LANES)).astype(BF16), lower, preferred_element_type=F32
        )
        passed = passed + jnp.sum(meets, axis=1, keepdims=True)
        after = jnp.where(row["after"], after_slot[0:1, :], -1.0).astype(jnp.int32)
        before = jnp.where(row["before"], before_slot[0:1, low], -1.0).astype(jnp.int32)
        near = jnp.where(even, after, before)
        far = jnp.where(even, before, after)
        slots_ref[0:1, low] = near
        slots_ref[1:2, low] = far
        high = slice(512 + k * LANES, 512 + (k + 1) * LANES)
        pack_ref[0:64, low] = pack_ref[64:128, high] = one_hot(slot == near)
        pack_ref[128:192, high] = pack_ref[192:256, low] = one_hot(slot == far)
        pack_ref[0:64, high] = pack_ref[64:128, low] = jnp.zeros((64, LANES), BF16)
        pack_ref[128:192, low] = pack_ref[192:256, high] = jnp.zeros((64, LANES), BF16)

def place_weights(rows, slots_ref, own_ref, halo_ref):
    number = lax.broadcasted_iota(jnp.int32, (512, LANES), 0)
    slot = lax.broadcasted_iota(jnp.int32, (64, LANES), 0)
    for k, row in enumerate(rows):
        low = slice(k * LANES, (k + 1) * LANES)
        high = slice(512 + k * LANES, 512 + (k + 1) * LANES)
        own_ref[:, low] = one_hot(number == jnp.where(row["own"], row["source"], -1))
        near = one_hot(slot == slots_ref[0:1, low])
        far = one_hot(slot == slots_ref[1:2, low])
        for again in (0, 128):
            halo_ref[again : again + 64, low] = near
            halo_ref[again + 64 : again + 128, low] = far
            halo_ref[again : again + 64, high] = far
            halo_ref[again + 64 : again + 128, high] = near


def split(value):
    top = value.astype(BF16)
    return top, (value - top.astype(F32)).astype(BF16)


def edges_out(state_ref, metric_ref, pack_ref, acc_ref, high_ref, low_ref, near_ref, far_refs, ready):
    flat = state_ref.reshape(2 * NVAR * LEV * 8, LANES)

    def metric(direction, point):
        row = 8 * (16 * direction + point)
        return metric_ref[row : row + 8, :]

    def group(index, carry):
        base = index * 64
        u = [
            flat[pl.ds(base + (p // 8) * (NVAR * LEV * 8) + p % 8, 8, stride=8), :] for p in range(16)
        ]
        tendency = scaled_tendency(u, metric)
        for p in range(16):
            if p in CORNERS:
                value = u[p]
            elif p in RIM_POINTS:
                value = u[p] + tendency[p]
            else:
                value = u[p] + 2.0 * tendency[p]
            acc_ref[pl.ds(pl.multiple_of(index * 128 + 8 * p, 8), 8), :] = value
        rows = pl.ds(pl.multiple_of(index * 16, 16), 16)
        for k in range(4):
            for half in range(2):
                first, second = EDGE_POINTS[k][2 * half : 2 * half + 2]
                place = slice(half * 512 + k * LANES, half * 512 + (k + 1) * LANES)
                top, rest = split(jnp.concatenate([tendency[first], tendency[second]], 0))
                high_ref[rows, place] = top
                low_ref[rows, place] = rest
        return carry

    def variable(var, carry):
        ready(var)
        def three(index, carry):
            for i in range(3):
                group(var * GROUPS + 3 * index + i, carry)
            return carry

        return lax.fori_loop(0, GROUPS // 3, three, carry)

    lax.fori_loop(0, NVAR, variable, 0)
    across = (((1,), (1,)), ((), ()))
    packed = lax.dot_general(
        high_ref[...], pack_ref[...], across, preferred_element_type=F32
    ) + lax.dot_general(low_ref[...], pack_ref[...], across, preferred_element_type=F32)
    near_ref[...] = packed[:, :LANES]
    far_refs[0][...] = packed[: 3 * 144, LANES:]
    far_refs[1][...] = packed[3 * 144 :, LANES:]


def first_kernel(devices, state_hbm, metric_hbm, peer_hbm, code_hbm, work_hbm,
                 peer_ref, code_ref, work_ref, slots_ref, acc_ref, high_ref, low_ref,
                 near_ref, far0_ref, far1_ref, state_ref, metric_ref, scaled_ref, hit_ref, less_ref, pack_ref, small_sems, sems):
    me = lax.axis_index(("elem", "col"))
    small = [
        pltpu.make_async_copy(source, target, small_sems.at[i])
        for i, (source, target) in enumerate(
            [(peer_hbm, peer_ref), (code_hbm, code_ref), (metric_hbm, metric_ref), (work_hbm, work_ref)]
        )
    ]

    def half_of(i, half):
        var = jnp.where(i < 3, i + 2, jnp.where(i < 5, i - 3, i))
        return pltpu.make_async_copy(
            state_hbm.at[pl.ds(var * LEV, LEV), pl.ds(8 * half, 8), :],
            state_ref.at[half, pl.ds(i * LEV, LEV)],
            sems.at[i, half],
        )

    def fetch(i):
        for half in range(2):
            half_of(i, half).start()

    for copy in small:
        copy.start()
    fetch(0)
    fetch(1)
    small[0].wait()
    small[1].wait()
    rows = edge_rows(peer_ref, code_ref, me, devices)
    slots_of(rows, lax.rem(me, 2) == 0, hit_ref, less_ref, pack_ref, slots_ref)
    small[2].wait()
    small[3].wait()
    for i in range(32):
        scaled_ref[8 * i : 8 * i + 8, :] = jnp.broadcast_to(
            metric_scale(i // 16, i % 16) * metric_ref[i : i + 1, :], (8, LANES)
        )

    def ready(i):
        for half in range(2):
            half_of(i, half).wait()

        @pl.when(i + AHEAD < NVAR)
        def _():
            fetch(i + AHEAD)

    for i in range(2, AHEAD):
        fetch(i)
    edges_out(state_ref, scaled_ref, pack_ref, acc_ref, high_ref, low_ref,
              near_ref, (far0_ref, far1_ref), ready)


def turned_edges(code_ref):
    return [
        jnp.broadcast_to(lax.bitwise_and(code_ref[k : k + 1, :], 1), (8, LANES)) == 1 for k in range(4)
    ]


def averaged(index, line_index, turned, acc_ref, lines_ref):
    base = index * 128
    value = [acc_ref[pl.ds(pl.multiple_of(base + 8 * p, 8), 8), :] for p in range(16)]
    for k in range(4):
        line = []
        for half in range(2):
            place = slice(half * 512 + k * LANES, half * 512 + (k + 1) * LANES)
            for second in range(2):
                rows = pl.ds(pl.multiple_of(line_index * 16 + 8 * second, 8), 8)
                line.append(lines_ref[rows, place])
        for t in range(4):
            p = EDGE_POINTS[k][t]
            value[p] = value[p] + jnp.where(turned[k], line[3 - t], line[t])
    return value


def second_kernel(devices, peer_ref, code_ref, slots_ref, acc_ref, high_ref, low_ref,
                  halo_ref, first_ref, rest_ref, own_ref, lines_ref):
    me = lax.axis_index(("elem", "col"))
    place_weights(edge_rows(peer_ref, code_ref, me, devices), slots_ref, own_ref, halo_ref)

    for half in range(2):
        place = slice(half * 512, (half + 1) * 512)
        lines_ref[:, place] = jnp.dot(
            high_ref[:, place], own_ref[...], preferred_element_type=F32
        ) + jnp.dot(low_ref[:, place], own_ref[...], preferred_element_type=F32)
    turned = turned_edges(code_ref)

    def group_into(out_ref, skipped):
        def group(index, carry):
            for p, value in enumerate(averaged(index, index, turned, acc_ref, lines_ref)):
                out_ref[pl.ds(pl.multiple_of((index - skipped * GROUPS) * 128 + 8 * p, 8), 8), :] = value
            return carry

        return group

    lax.fori_loop(0, 3 * GROUPS, group_into(first_ref, 0), 0, unroll=3)
    lax.fori_loop(3 * GROUPS, NVAR * GROUPS, group_into(rest_ref, 3), 0, unroll=3)


LOG2E = float(np.log2(np.e))


def softplus2(y):
    tail = jnp.exp2(jnp.minimum(y, -y))
    small = tail * (LOG2E - (0.5 * LOG2E) * tail)
    return jnp.maximum(y, 0.0) + jnp.where(tail < 1e-3, small, jnp.log2(1.0 + tail))


UNROLL = 8


def level(half, var, number):
    return pl.ds((half * 3 + var) * (LEV * 8) + number, 8)


def physics(dyn_ref, mark_ref):
    work = [mark_ref[8 * half : 8 * half + 8, :] for half in range(2)]
    marks = [[jnp.where(w >= section, 1.0, 0.0) for section in (1, 2, 3)] for w in work]

    def condense(block, rain):
        base = pl.multiple_of(block * (8 * UNROLL), 8)
        rain = list(rain)
        for step in range(UNROLL):
            for half in range(2):
                heat_at, vapour_at, water_at = [level(half, var, base + 8 * step) for var in range(3)]
                heat = dyn_ref[heat_at, :]
                vapour = dyn_ref[vapour_at, :]
                excess = LOG2E * vapour - (0.5 * LOG2E) * heat
                total = None
                for mark in marks[half]:
                    amount = mark * softplus2(excess)
                    excess = excess - (1.25 * 0.3) * amount
                    total = amount if total is None else total + amount
                total = (0.3 / LOG2E) * total
                dyn_ref[heat_at, :] = heat + 0.5 * total
                dyn_ref[vapour_at, :] = vapour - total
                dyn_ref[water_at, :] = dyn_ref[water_at, :] + total
                rain[half] = rain[half] + total
        return tuple(rain)

    zero = jnp.zeros((8, LANES), F32)
    return jnp.concatenate(lax.fori_loop(0, LEV // UNROLL, condense, (zero, zero)), axis=0)


def mixed(var, dyn_ref, out_ref):
    for half in range(2):

        def at(number, half=half):
            return dyn_ref[level(half, var, 8 * number), :]

        here = at(0)
        above = here + here
        for number in range(LEV):
            lower = at(min(number + 1, LEV - 1))
            below = here + lower
            out_ref[level(half, var, 8 * number), :] = 0.25 * (above + below)
            here, above = lower, below


def by_span(rain):
    point = lax.broadcasted_iota(jnp.int32, (16, LANES), 0)
    eighth = lax.shift_right_logical(lax.broadcasted_iota(jnp.int32, (16, LANES), 1), 3)
    total = None
    for shift in range(16):
        moved = pltpu.roll(rain, 8 * shift, 1) if shift else rain
        kept = jnp.where(point == eighth, moved, 0.0)
        kept = pltpu.roll(kept, 16 - shift, 0) if shift else kept
        total = kept if total is None else total + kept
    return total


def halo_lines(first, near_ref, far_ref, halo_ref, lines_ref):
    rows = slice(first * 144, first * 144 + far_ref.shape[0])
    lane = lax.broadcasted_iota(jnp.int32, far_ref.shape, 1)
    for half in range(2):
        low, high = near_ref[rows, :], far_ref[...]
        if half:
            low, high = high, low
        halo = jnp.concatenate(split(jnp.where(lane < 64, low, high)), axis=1)
        place = slice(half * 512, (half + 1) * 512)
        lines_ref[:, place] = jnp.dot(halo, halo_ref[:, place], preferred_element_type=F32)


def leave(i, source, source_at, state_out, sems):
    return [
        pltpu.make_async_copy(
            source.at[half, pl.ds(source_at * LEV, LEV)],
            state_out.at[pl.ds(ORDER[i] * LEV, LEV), pl.ds(8 * half, 8), :],
            sems.at[2 * i + half],
        )
        for half in range(2)
    ]


def into_halves(index, count, values, flat):
    for p, value in enumerate(values):
        flat[pl.ds(index * 64 + (p // 8) * (count * LEV * 8) + p % 8, 8, stride=8), :] = value


def third_kernel(owner_ref, code_ref, mark_ref, acc_ref, halo_ref, near_ref, far_ref,
                 mixed_ref, rain_ref,
                 lines_ref, dyn_ref, rain_rows, counts):
    halo_lines(0, near_ref, far_ref, halo_ref, lines_ref)
    turned = turned_edges(code_ref)
    flat = dyn_ref.reshape(2 * 3 * LEV * 8, LANES)
    flat_out = mixed_ref.reshape(2 * 3 * LEV * 8, LANES)

    def group(index, carry):
        into_halves(index, 3, averaged(index, index, turned, acc_ref, lines_ref), flat)
        return carry

    lax.fori_loop(0, 3 * GROUPS, group, 0, unroll=3)
    rain = physics(flat, mark_ref)
    for var in range(3):
        mixed(var, flat, flat_out)
    rain_rows[...] = by_span(rain) * (1.0 / LEV)
    rain_ref[...] = jnp.zeros_like(rain_ref)
    for owner in range(8):
        counts[owner] = 0
    for span in range(16):
        owner = owner_ref[span]
        rank = counts[owner]
        counts[owner] = rank + 1
        rain_ref[owner, pl.ds(rank, 1), :] = rain_rows[span : span + 1, :]


def fourth_kernel(code_ref, acc_hbm, halo_ref, near_ref, far_ref, mixed_ref, state_out,
                  lines_ref, acc_ref, dyn_ref, in_sems, sems):
    count = NVAR - 3
    held = [
        pltpu.make_async_copy(
            acc_hbm.at[pl.ds(i * ROWS, ROWS)], acc_ref.at[pl.ds(i * ROWS, ROWS)], in_sems.at[i]
        )
        for i in range(count)
    ]
    for copy in held:
        copy.start()
    halo_lines(3, near_ref, far_ref, halo_ref, lines_ref)
    turned = turned_edges(code_ref)
    flat = dyn_ref.reshape(2 * count * LEV * 8, LANES)

    def group(index, carry):
        into_halves(index, count, averaged(index, index, turned, acc_ref, lines_ref), flat)
        return carry

    copies = sum([leave(i, mixed_ref, i, state_out, sems) for i in range(3)], [])
    for copy in copies:
        copy.start()
    for i in range(count):
        held[i].wait()
        lax.fori_loop(i * GROUPS, (i + 1) * GROUPS, group, 0, unroll=3)
        for copy in leave(i + 3, dyn_ref, i, state_out, sems):
            copy.start()
            copies.append(copy)
    for copy in copies:
        copy.wait()


def swapped(value, axes, partner):
    count = lax.axis_size(axes)
    return lax.ppermute(value, axes, [(source, partner(source, count)) for source in range(count)])


def near_partner(source, count):
    return source + 1 if source % 2 == 0 else source - 1


def far_partner(source, count):
    return (source - 1) % count if source % 2 == 0 else (source + 1) % count


VM = pl.BlockSpec(memory_space=pltpu.VMEM)
SM = pl.BlockSpec(memory_space=pltpu.SMEM)
HB = pl.BlockSpec(memory_space=pltpu.HBM)


def shape(*sizes, dtype=F32):
    return jax.ShapeDtypeStruct(sizes, dtype)


def call(kernel, out, ins, outs, scratch, cost, **more):
    return pl.pallas_call(
        kernel,
        out_shape=out,
        in_specs=ins,
        out_specs=outs,
        scratch_shapes=scratch,
        cost_estimate=pl.CostEstimate(flops=cost, bytes_accessed=cost // 1000, transcendentals=0),
        compiler_params=pltpu.CompilerParams(vmem_limit_bytes=VMEM_LIMIT),
        **more,
    )


def in_hbm(value):
    return pltpu.with_memory_space_constraint(value, pltpu.HBM)


def body(state, metric, edge_peer, edge_code, span_owner, work_class):
    axes = ("elem", "col")
    devices = lax.axis_size(axes)
    state = state.reshape(NVAR * LEV, 16, LANES)
    metric = metric.reshape(32, LANES)
    owner = span_owner.reshape(16)
    count = NVAR - 3
    peer, code, work, slots, acc, high, low, near, far0, far1 = call(
        lambda *refs: first_kernel(devices, *refs),
        [
            shape(4, LANES, dtype=jnp.int32),
            shape(4, LANES, dtype=jnp.int32),
            shape(16, LANES, dtype=jnp.int32),
            shape(8, 512, dtype=jnp.int32),
            shape(NVAR * ROWS, LANES),
            shape(LINES, 1024, dtype=BF16),
            shape(LINES, 1024, dtype=BF16),
            shape(LINES, LANES),
            shape(3 * 144, LANES),
            shape(count * 144, LANES),
        ],
        [HB] * 5,
        [VM] * 10,
        [
            pltpu.VMEM((2, NVAR * LEV, 8, LANES), F32),
            pltpu.VMEM((32, LANES), F32),
            pltpu.VMEM((256, LANES), F32),
            pltpu.VMEM((512, 512), BF16),
            pltpu.VMEM((512, 512), BF16),
            pltpu.VMEM((256, 1024), BF16),
            pltpu.SemaphoreType.DMA((4,)),
            pltpu.SemaphoreType.DMA((NVAR, 2)),
        ],
        2_000_000_000,
    )(in_hbm(state), in_hbm(metric), in_hbm(edge_peer), in_hbm(edge_code), in_hbm(work_class))
    from_far0 = swapped(far0, axes, far_partner)
    from_near = swapped(near, axes, near_partner)
    from_far1 = swapped(far1, axes, far_partner)
    halo, acc, acc_rest = call(
        lambda *refs: second_kernel(devices, *refs),
        [shape(256, 1024, dtype=BF16), shape(3 * ROWS, LANES), shape(count * ROWS, LANES)],
        [VM] * 6,
        [VM] * 3,
        [
            pltpu.VMEM((512, 512), BF16),
            pltpu.VMEM((LINES, 1024), F32),
        ],
        4_000_000_000,
    )(peer, code, slots, acc, high, low)
    mixed1, rain = call(
        third_kernel,
        [shape(2, 3 * LEV, 8, LANES), shape(8, CAP, LANES)],
        [SM] + [VM] * 6,
        [VM, VM],
        [
            pltpu.VMEM((3 * 144, 1024), F32),
            pltpu.VMEM((2, 3 * LEV, 8, LANES), F32),
            pltpu.VMEM((16, LANES), F32),
            pltpu.SMEM((8,), jnp.int32),
        ],
        2_000_000_000,
    )(owner, code, work, acc, halo, from_near, from_far0)
    rain = lax.all_to_all(rain, "col", split_axis=0, concat_axis=0, tiled=True)
    new_state = call(
        fourth_kernel,
        shape(NVAR * LEV, 16, LANES),
        [VM, HB] + [VM] * 4,
        HB,
        [
            pltpu.VMEM((count * 144, 1024), F32),
            pltpu.VMEM((count * ROWS, LANES), F32),
            pltpu.VMEM((2, count * LEV, 8, LANES), F32),
            pltpu.SemaphoreType.DMA((count,)),
            pltpu.SemaphoreType.DMA((2 * NVAR,)),
        ],
        10_000_000_000,
    )(code, in_hbm(acc_rest), halo, from_near, from_far1, mixed1)
    new_state, rain = lax.optimization_barrier((new_state, rain))
    return new_state.reshape(NVAR, LEV, 16, LANES), rain.reshape(1, 1, 8 * CAP, LANES)


def solution(mesh):
    placed = (
        P(None, None, None, ("elem", "col")),
        P(None, None, ("elem", "col")),
        P(None, ("elem", "col")),
        P(None, ("elem", "col")),
        P(("elem", "col"), None),
        P(None, ("elem", "col")),
    )
    return jax.shard_map(
        body,
        mesh=mesh,
        in_specs=placed,
        out_specs=(P(None, None, None, ("elem", "col")), P("elem", "col", None, None)),
        check_vma=False,
    )
```

```python
import jax
import jax.numpy as jnp
import numpy as np
from jax import lax
from jax.experimental import pallas as pl
from jax.experimental.pallas import tpu as pltpu
from jax.sharding import PartitionSpec as P

LEV = 72
GROUPS = LEV // 8
ROWS = LEV * 16
LANES = 128
EDGE_POINTS = ((0, 1, 2, 3), (3, 7, 11, 15), (12, 13, 14, 15), (0, 4, 8, 12))
RIM_POINTS = (0, 1, 2, 3, 4, 7, 8, 11, 12, 13, 14, 15)
CORNERS = (0, 3, 12, 15)
SCALE = 0.5 * 0.03
ORDER = (2, 3, 4, 0, 1, 5, 6)
NVAR = 7
AHEAD = 2
LINES = NVAR * GROUPS * 16
CAP = 3
F32 = jnp.float32
BF16 = jnp.bfloat16
VMEM_LIMIT = 20 * 1024 * 1024


def derivative_matrix():
    nodes = np.array([-1.0, -1.0 / np.sqrt(5.0), 1.0 / np.sqrt(5.0), 1.0])
    weights = np.array(
        [1.0 / np.prod([nodes[a] - nodes[b] for b in range(4) if b != a]) for a in range(4)]
    )
    table = np.zeros((4, 4))
    for a in range(4):
        for b in range(4):
            if a != b:
                table[a, b] = weights[b] / weights[a] / (nodes[a] - nodes[b])
        table[a, a] = -table[a].sum()
    return table


DG = derivative_matrix()
EVEN0 = float((DG[0, 0] + DG[0, 3]) / 2)
EVEN1 = float((DG[1, 0] + DG[1, 3]) / 2)
ODD00 = float((DG[0, 0] - DG[0, 3]) / 2)
ODD01 = float((DG[0, 1] - DG[0, 2]) / 2)
ODD10 = float((DG[1, 0] - DG[1, 3]) / 2)
ODD11 = float((DG[1, 1] - DG[1, 2]) / 2)


def derive_fluxes(u0, u1, u2, u3):
    even = (u0 + u3) - (u1 + u2)
    o0 = u0 - u3
    o1 = u1 - u2
    b0 = (ODD00 / EVEN0) * o0 + (ODD01 / EVEN0) * o1
    b1 = (ODD10 / EVEN1) * o0 + (ODD11 / EVEN1) * o1
    return even + b0, even + b1, b1 - even, b0 - even


def derive_again(u0, u1, u2, u3):
    even = (u0 + u3) - (u1 + u2)
    o0 = u0 - u3
    o1 = u1 - u2
    a1 = (EVEN1 / EVEN0) * even
    b0 = (ODD00 / EVEN0) * o0 + (ODD01 / EVEN0) * o1
    b1 = (ODD10 / EVEN0) * o0 + (ODD11 / EVEN0) * o1
    return even + b0, a1 + b1, b1 - a1, b0 - even


def metric_scale(direction, point):
    row = (point // 4, point % 4)[1 - direction]
    return SCALE * EVEN0 * (EVEN0, EVEN1, EVEN1, EVEN0)[row]


def scaled_tendency(u, metric):
    total = [None] * 16
    for b in range(4):
        points = [4 * b + a for a in range(4)]
        flux = derive_fluxes(*[u[p] for p in points])
        for p, value in zip(points, derive_again(*[f * metric(0, p) for f, p in zip(flux, points)])):
            total[p] = value
    for a in range(4):
        points = [a + 4 * b for b in range(4)]
        flux = derive_fluxes(*[u[p] for p in points])
        for p, value in zip(points, derive_again(*[f * metric(1, p) for f, p in zip(flux, points)])):
            total[p] = total[p] + value
    return total


def edge_rows(peer_ref, code_ref, me, devices):
    rows = []
    for k in range(4):
        peer = peer_ref[k : k + 1, :]
        code = code_ref[k : k + 1, :]
        offset = lax.shift_right_logical(peer, 7) - me
        source = lax.shift_right_logical(code, 1) * LANES + lax.bitwise_and(peer, LANES - 1)
        rows.append(
            dict(
                source=source,
                own=offset == 0,
                after=(offset == 1) | (offset == 1 - devices),
                before=(offset == -1) | (offset == devices - 1),
            )
        )
    return rows


def one_hot(mask):
    return jnp.where(mask, 1.0, 0.0).astype(BF16)


def slots_of(rows, even, hit_ref, less_ref, pack_ref, slots_ref):
    number = lax.broadcasted_iota(jnp.int32, (LANES, LANES), 0)
    line = lax.broadcasted_iota(jnp.int32, (16, LANES), 0)
    for k, row in enumerate(rows):
        low = slice(k * LANES, (k + 1) * LANES)
        hit_ref[:, low] = one_hot((line == lax.shift_right_logical(row["source"], 7)) & row["before"])
        less_ref[:, low] = one_hot(number == lax.bitwise_and(row["source"], LANES - 1))
    met = lax.dot_general(
        hit_ref[...], less_ref[...], (((1,), (1,)), ((), ())), preferred_element_type=F32
    )
    lower = one_hot(number < lax.broadcasted_iota(jnp.int32, (LANES, LANES), 1))
    sums = jnp.sum(met, axis=1, keepdims=True)
    counted = jnp.dot(met.astype(BF16), lower, preferred_element_type=F32)
    for k in range(3):
        counted = counted + jnp.where(line > k, sums[k : k + 1, :], 0.0)
    sent = jnp.dot(counted.astype(BF16), less_ref[...], preferred_element_type=F32)
    passed = jnp.zeros((1, 1), F32)
    slot = lax.broadcasted_iota(jnp.int32, (64, LANES), 0)
    for k, row in enumerate(rows):
        low = slice(k * LANES, (k + 1) * LANES)
        meets = jnp.where(row["after"], 1.0, 0.0)
        after_slot = passed + jnp.dot(
            jnp.broadcast_to(meets, (16, LANES)).astype(BF16), lower, preferred_element_type=F32
        )
        passed = passed + jnp.sum(meets, axis=1, keepdims=True)
        after = jnp.where(row["after"], after_slot[0:1, :], -1.0).astype(jnp.int32)
        own_line = line == lax.shift_right_logical(row["source"], 7)
        before_slot = jnp.sum(jnp.where(own_line, sent[:, low], 0.0), axis=0, keepdims=True)
        before = jnp.where(row["before"], before_slot, -1.0).astype(jnp.int32)
        near = jnp.where(even, after, before)
        far = jnp.where(even, before, after)
        slots_ref[0:1, low] = near
        slots_ref[1:2, low] = far
        high = slice(512 + k * LANES, 512 + (k + 1) * LANES)
        pack_ref[0:64, low] = pack_ref[64:128, high] = one_hot(slot == near)
        pack_ref[128:192, high] = pack_ref[192:256, low] = one_hot(slot == far)
        pack_ref[0:64, high] = pack_ref[64:128, low] = jnp.zeros((64, LANES), BF16)
        pack_ref[128:192, low] = pack_ref[192:256, high] = jnp.zeros((64, LANES), BF16)

def place_weights(rows, slots_ref, own_ref, halo_ref):
    number = lax.broadcasted_iota(jnp.int32, (512, LANES), 0)
    slot = lax.broadcasted_iota(jnp.int32, (64, LANES), 0)
    for k, row in enumerate(rows):
        low = slice(k * LANES, (k + 1) * LANES)
        high = slice(512 + k * LANES, 512 + (k + 1) * LANES)
        own_ref[:, low] = one_hot(number == jnp.where(row["own"], row["source"], -1))
        near = one_hot(slot == slots_ref[0:1, low])
        far = one_hot(slot == slots_ref[1:2, low])
        for again in (0, 128):
            halo_ref[again : again + 64, low] = near
            halo_ref[again + 64 : again + 128, low] = far
            halo_ref[again : again + 64, high] = far
            halo_ref[again + 64 : again + 128, high] = near


def split(value):
    top = value.astype(BF16)
    return top, (value - top.astype(F32)).astype(BF16)


def edges_out(state_ref, metric_ref, pack_ref, acc_ref, high_ref, low_ref, near_ref, far_refs, ready):
    flat = state_ref.reshape(2 * NVAR * LEV * 8, LANES)

    def metric(direction, point):
        row = 8 * (16 * direction + point)
        return metric_ref[row : row + 8, :]

    def group(index, carry):
        base = index * 64
        u = [
            flat[pl.ds(base + (p // 8) * (NVAR * LEV * 8) + p % 8, 8, stride=8), :] for p in range(16)
        ]
        tendency = scaled_tendency(u, metric)
        for p in range(16):
            if p in CORNERS:
                value = u[p]
            elif p in RIM_POINTS:
                value = u[p] + tendency[p]
            else:
                value = u[p] + 2.0 * tendency[p]
            acc_ref[pl.ds(pl.multiple_of(index * 128 + 8 * p, 8), 8), :] = value
        rows = pl.ds(pl.multiple_of(index * 16, 16), 16)
        for k in range(4):
            for half in range(2):
                first, second = EDGE_POINTS[k][2 * half : 2 * half + 2]
                place = slice(half * 512 + k * LANES, half * 512 + (k + 1) * LANES)
                top, rest = split(jnp.concatenate([tendency[first], tendency[second]], 0))
                high_ref[rows, place] = top
                low_ref[rows, place] = rest
        return carry

    def variable(var, carry):
        ready(var)
        def three(index, carry):
            for i in range(3):
                group(var * GROUPS + 3 * index + i, carry)
            return carry

        return lax.fori_loop(0, GROUPS // 3, three, carry)

    lax.fori_loop(0, NVAR, variable, 0)
    across = (((1,), (1,)), ((), ()))
    packed = lax.dot_general(
        high_ref[...], pack_ref[...], across, preferred_element_type=F32
    ) + lax.dot_general(low_ref[...], pack_ref[...], across, preferred_element_type=F32)
    near_ref[...] = packed[:, :LANES]
    far_refs[0][...] = packed[: 3 * 144, LANES:]
    far_refs[1][...] = packed[3 * 144 :, LANES:]


def first_kernel(devices, state_hbm, metric_hbm, peer_hbm, code_hbm, work_hbm,
                 peer_ref, code_ref, work_ref, slots_ref, acc_ref, high_ref, low_ref,
                 near_ref, far0_ref, far1_ref, state_ref, metric_ref, scaled_ref, hit_ref, less_ref, pack_ref, small_sems, sems):
    me = lax.axis_index(("elem", "col"))
    small = [
        pltpu.make_async_copy(source, target, small_sems.at[i])
        for i, (source, target) in enumerate(
            [(peer_hbm, peer_ref), (code_hbm, code_ref), (metric_hbm, metric_ref), (work_hbm, work_ref)]
        )
    ]

    def half_of(i, half):
        var = jnp.where(i < 3, i + 2, jnp.where(i < 5, i - 3, i))
        return pltpu.make_async_copy(
            state_hbm.at[pl.ds(var * LEV, LEV), pl.ds(8 * half, 8), :],
            state_ref.at[half, pl.ds(i * LEV, LEV)],
            sems.at[i, half],
        )

    def fetch(i):
        for half in range(2):
            half_of(i, half).start()

    for copy in small:
        copy.start()
    fetch(0)
    fetch(1)
    small[0].wait()
    small[1].wait()
    rows = edge_rows(peer_ref, code_ref, me, devices)
    slots_of(rows, lax.rem(me, 2) == 0, hit_ref, less_ref, pack_ref, slots_ref)
    small[2].wait()
    small[3].wait()
    for i in range(32):
        scaled_ref[8 * i : 8 * i + 8, :] = jnp.broadcast_to(
            metric_scale(i // 16, i % 16) * metric_ref[i : i + 1, :], (8, LANES)
        )

    def ready(i):
        for half in range(2):
            half_of(i, half).wait()

        @pl.when(i + AHEAD < NVAR)
        def _():
            fetch(i + AHEAD)

    for i in range(2, AHEAD):
        fetch(i)
    edges_out(state_ref, scaled_ref, pack_ref, acc_ref, high_ref, low_ref,
              near_ref, (far0_ref, far1_ref), ready)


def turned_edges(code_ref):
    return [
        jnp.broadcast_to(lax.bitwise_and(code_ref[k : k + 1, :], 1), (8, LANES)) == 1 for k in range(4)
    ]


def averaged(index, line_index, turned, acc_ref, lines_ref):
    base = index * 128
    value = [acc_ref[pl.ds(pl.multiple_of(base + 8 * p, 8), 8), :] for p in range(16)]
    for k in range(4):
        line = []
        for half in range(2):
            place = slice(half * 512 + k * LANES, half * 512 + (k + 1) * LANES)
            for second in range(2):
                rows = pl.ds(pl.multiple_of(line_index * 16 + 8 * second, 8), 8)
                line.append(lines_ref[rows, place])
        for t in range(4):
            p = EDGE_POINTS[k][t]
            value[p] = value[p] + jnp.where(turned[k], line[3 - t], line[t])
    return value


def second_kernel(devices, peer_ref, code_ref, slots_ref, acc_ref, high_ref, low_ref,
                  halo_ref, first_ref, rest_ref, own_ref, lines_ref):
    me = lax.axis_index(("elem", "col"))
    place_weights(edge_rows(peer_ref, code_ref, me, devices), slots_ref, own_ref, halo_ref)

    for half in range(2):
        place = slice(half * 512, (half + 1) * 512)
        lines_ref[:, place] = jnp.dot(
            high_ref[:, place], own_ref[...], preferred_element_type=F32
        ) + jnp.dot(low_ref[:, place], own_ref[...], preferred_element_type=F32)
    turned = turned_edges(code_ref)

    def group_into(out_ref, skipped):
        def group(index, carry):
            for p, value in enumerate(averaged(index, index, turned, acc_ref, lines_ref)):
                out_ref[pl.ds(pl.multiple_of((index - skipped * GROUPS) * 128 + 8 * p, 8), 8), :] = value
            return carry

        return group

    lax.fori_loop(0, 3 * GROUPS, group_into(first_ref, 0), 0, unroll=3)
    lax.fori_loop(3 * GROUPS, NVAR * GROUPS, group_into(rest_ref, 3), 0, unroll=3)


LOG2E = float(np.log2(np.e))


def softplus2(y):
    tail = jnp.exp2(jnp.minimum(y, -y))
    small = tail * (LOG2E - (0.5 * LOG2E) * tail)
    return jnp.maximum(y, 0.0) + jnp.where(tail < 1e-3, small, jnp.log2(1.0 + tail))


UNROLL = 8


def level(half, var, number):
    return pl.ds((half * 3 + var) * (LEV * 8) + number, 8)


def physics(dyn_ref, mark_ref):
    work = [mark_ref[8 * half : 8 * half + 8, :] for half in range(2)]
    marks = [[jnp.where(w >= section, 1.0, 0.0) for section in (1, 2, 3)] for w in work]

    def condense(block, rain):
        base = pl.multiple_of(block * (8 * UNROLL), 8)
        rain = list(rain)
        for step in range(UNROLL):
            for half in range(2):
                heat_at, vapour_at, water_at = [level(half, var, base + 8 * step) for var in range(3)]
                heat = dyn_ref[heat_at, :]
                vapour = dyn_ref[vapour_at, :]
                excess = LOG2E * vapour - (0.5 * LOG2E) * heat
                total = None
                for mark in marks[half]:
                    amount = mark * softplus2(excess)
                    excess = excess - (1.25 * 0.3) * amount
                    total = amount if total is None else total + amount
                total = (0.3 / LOG2E) * total
                dyn_ref[heat_at, :] = heat + 0.5 * total
                dyn_ref[vapour_at, :] = vapour - total
                dyn_ref[water_at, :] = dyn_ref[water_at, :] + total
                rain[half] = rain[half] + total
        return tuple(rain)

    zero = jnp.zeros((8, LANES), F32)
    return jnp.concatenate(lax.fori_loop(0, LEV // UNROLL, condense, (zero, zero)), axis=0)


def mixed(var, dyn_ref, out_ref):
    for half in range(2):

        def at(number, half=half):
            return dyn_ref[level(half, var, 8 * number), :]

        here = at(0)
        above = here + here
        for number in range(LEV):
            lower = at(min(number + 1, LEV - 1))
            below = here + lower
            out_ref[level(half, var, 8 * number), :] = 0.25 * (above + below)
            here, above = lower, below


def by_span(rain):
    point = lax.broadcasted_iota(jnp.int32, (16, LANES), 0)
    eighth = lax.shift_right_logical(lax.broadcasted_iota(jnp.int32, (16, LANES), 1), 3)
    total = None
    for shift in range(16):
        moved = pltpu.roll(rain, 8 * shift, 1) if shift else rain
        kept = jnp.where(point == eighth, moved, 0.0)
        kept = pltpu.roll(kept, 16 - shift, 0) if shift else kept
        total = kept if total is None else total + kept
    return total


def halo_lines(first, near_ref, far_ref, halo_ref, lines_ref):
    rows = slice(first * 144, first * 144 + far_ref.shape[0])
    lane = lax.broadcasted_iota(jnp.int32, far_ref.shape, 1)
    for half in range(2):
        low, high = near_ref[rows, :], far_ref[...]
        if half:
            low, high = high, low
        halo = jnp.concatenate(split(jnp.where(lane < 64, low, high)), axis=1)
        place = slice(half * 512, (half + 1) * 512)
        lines_ref[:, place] = jnp.dot(halo, halo_ref[:, place], preferred_element_type=F32)


def leave(i, source, source_at, state_out, sems):
    return [
        pltpu.make_async_copy(
            source.at[half, pl.ds(source_at * LEV, LEV)],
            state_out.at[pl.ds(ORDER[i] * LEV, LEV), pl.ds(8 * half, 8), :],
            sems.at[2 * i + half],
        )
        for half in range(2)
    ]


def into_halves(index, count, values, flat):
    for p, value in enumerate(values):
        flat[pl.ds(index * 64 + (p // 8) * (count * LEV * 8) + p % 8, 8, stride=8), :] = value


def third_kernel(owner_ref, code_ref, mark_ref, acc_ref, halo_ref, near_ref, far_ref,
                 mixed_ref, rain_ref,
                 lines_ref, dyn_ref, rain_rows, counts):
    halo_lines(0, near_ref, far_ref, halo_ref, lines_ref)
    turned = turned_edges(code_ref)
    flat = dyn_ref.reshape(2 * 3 * LEV * 8, LANES)
    flat_out = mixed_ref.reshape(2 * 3 * LEV * 8, LANES)

    def group(index, carry):
        into_halves(index, 3, averaged(index, index, turned, acc_ref, lines_ref), flat)
        return carry

    lax.fori_loop(0, 3 * GROUPS, group, 0, unroll=3)
    rain = physics(flat, mark_ref)
    for var in range(3):
        mixed(var, flat, flat_out)
    rain_rows[...] = by_span(rain) * (1.0 / LEV)
    rain_ref[...] = jnp.zeros_like(rain_ref)
    for owner in range(8):
        counts[owner] = 0
    for span in range(16):
        owner = owner_ref[span]
        rank = counts[owner]
        counts[owner] = rank + 1
        rain_ref[owner, pl.ds(rank, 1), :] = rain_rows[span : span + 1, :]


def fourth_kernel(code_ref, acc_hbm, halo_ref, near_ref, far_ref, mixed_ref, state_out,
                  lines_ref, acc_ref, dyn_ref, in_sems, sems):
    count = NVAR - 3
    held = [
        pltpu.make_async_copy(
            acc_hbm.at[pl.ds(i * ROWS, ROWS)], acc_ref.at[pl.ds(i * ROWS, ROWS)], in_sems.at[i]
        )
        for i in range(count)
    ]
    for copy in held:
        copy.start()
    halo_lines(3, near_ref, far_ref, halo_ref, lines_ref)
    turned = turned_edges(code_ref)
    flat = dyn_ref.reshape(2 * count * LEV * 8, LANES)

    def group(index, carry):
        into_halves(index, count, averaged(index, index, turned, acc_ref, lines_ref), flat)
        return carry

    copies = sum([leave(i, mixed_ref, i, state_out, sems) for i in range(3)], [])
    for copy in copies:
        copy.start()
    for i in range(count):
        held[i].wait()
        lax.fori_loop(i * GROUPS, (i + 1) * GROUPS, group, 0, unroll=3)
        for copy in leave(i + 3, dyn_ref, i, state_out, sems):
            copy.start()
            copies.append(copy)
    for copy in copies:
        copy.wait()


def swapped(value, axes, partner):
    count = lax.axis_size(axes)
    return lax.ppermute(value, axes, [(source, partner(source, count)) for source in range(count)])


def near_partner(source, count):
    return source + 1 if source % 2 == 0 else source - 1


def far_partner(source, count):
    return (source - 1) % count if source % 2 == 0 else (source + 1) % count


VM = pl.BlockSpec(memory_space=pltpu.VMEM)
SM = pl.BlockSpec(memory_space=pltpu.SMEM)
HB = pl.BlockSpec(memory_space=pltpu.HBM)


def shape(*sizes, dtype=F32):
    return jax.ShapeDtypeStruct(sizes, dtype)


def call(kernel, out, ins, outs, scratch, cost, **more):
    return pl.pallas_call(
        kernel,
        out_shape=out,
        in_specs=ins,
        out_specs=outs,
        scratch_shapes=scratch,
        cost_estimate=pl.CostEstimate(flops=cost, bytes_accessed=cost // 1000, transcendentals=0),
        compiler_params=pltpu.CompilerParams(vmem_limit_bytes=VMEM_LIMIT),
        **more,
    )


def in_hbm(value):
    return pltpu.with_memory_space_constraint(value, pltpu.HBM)


def body(state, metric, edge_peer, edge_code, span_owner, work_class):
    axes = ("elem", "col")
    devices = lax.axis_size(axes)
    state = state.reshape(NVAR * LEV, 16, LANES)
    metric = metric.reshape(32, LANES)
    owner = span_owner.reshape(16)
    count = NVAR - 3
    peer, code, work, slots, acc, high, low, near, far0, far1 = call(
        lambda *refs: first_kernel(devices, *refs),
        [
            shape(4, LANES, dtype=jnp.int32),
            shape(4, LANES, dtype=jnp.int32),
            shape(16, LANES, dtype=jnp.int32),
            shape(8, 512, dtype=jnp.int32),
            shape(NVAR * ROWS, LANES),
            shape(LINES, 1024, dtype=BF16),
            shape(LINES, 1024, dtype=BF16),
            shape(LINES, LANES),
            shape(3 * 144, LANES),
            shape(count * 144, LANES),
        ],
        [HB] * 5,
        [VM] * 10,
        [
            pltpu.VMEM((2, NVAR * LEV, 8, LANES), F32),
            pltpu.VMEM((32, LANES), F32),
            pltpu.VMEM((256, LANES), F32),
            pltpu.VMEM((16, 512), BF16),
            pltpu.VMEM((LANES, 512), BF16),
            pltpu.VMEM((256, 1024), BF16),
            pltpu.SemaphoreType.DMA((4,)),
            pltpu.SemaphoreType.DMA((NVAR, 2)),
        ],
        2_000_000_000,
    )(in_hbm(state), in_hbm(metric), in_hbm(edge_peer), in_hbm(edge_code), in_hbm(work_class))
    from_far0 = swapped(far0, axes, far_partner)
    from_near = swapped(near, axes, near_partner)
    from_far1 = swapped(far1, axes, far_partner)
    halo, acc, acc_rest = call(
        lambda *refs: second_kernel(devices, *refs),
        [shape(256, 1024, dtype=BF16), shape(3 * ROWS, LANES), shape(count * ROWS, LANES)],
        [VM] * 6,
        [VM] * 3,
        [
            pltpu.VMEM((512, 512), BF16),
            pltpu.VMEM((LINES, 1024), F32),
        ],
        4_000_000_000,
    )(peer, code, slots, acc, high, low)
    mixed1, rain = call(
        third_kernel,
        [shape(2, 3 * LEV, 8, LANES), shape(8, CAP, LANES)],
        [SM] + [VM] * 6,
        [VM, VM],
        [
            pltpu.VMEM((3 * 144, 1024), F32),
            pltpu.VMEM((2, 3 * LEV, 8, LANES), F32),
            pltpu.VMEM((16, LANES), F32),
            pltpu.SMEM((8,), jnp.int32),
        ],
        2_000_000_000,
    )(owner, code, work, acc, halo, from_near, from_far0)
    rain = lax.all_to_all(rain, "col", split_axis=0, concat_axis=0, tiled=True)
    new_state = call(
        fourth_kernel,
        shape(NVAR * LEV, 16, LANES),
        [VM, HB] + [VM] * 4,
        HB,
        [
            pltpu.VMEM((count * 144, 1024), F32),
            pltpu.VMEM((count * ROWS, LANES), F32),
            pltpu.VMEM((2, count * LEV, 8, LANES), F32),
            pltpu.SemaphoreType.DMA((count,)),
            pltpu.SemaphoreType.DMA((2 * NVAR,)),
        ],
        10_000_000_000,
    )(code, in_hbm(acc_rest), halo, from_near, from_far1, mixed1)
    new_state, rain = lax.optimization_barrier((new_state, rain))
    return new_state.reshape(NVAR, LEV, 16, LANES), rain.reshape(1, 1, 8 * CAP, LANES)


def solution(mesh):
    placed = (
        P(None, None, None, ("elem", "col")),
        P(None, None, ("elem", "col")),
        P(None, ("elem", "col")),
        P(None, ("elem", "col")),
        P(("elem", "col"), None),
        P(None, ("elem", "col")),
    )
    return jax.shard_map(
        body,
        mesh=mesh,
        in_specs=placed,
        out_specs=(P(None, None, None, ("elem", "col")), P("elem", "col", None, None)),
        check_vma=False,
    )
```
